256 devices in a mesh: pert: 2 (over x_lo), band: 16 (over z, core), pw: 8 (over x_hi, y).
Axes of the slice: x: 4 (x_hi: 2, x_lo: 2; x = x_hi * 2 + x_lo), y: 4, z: 8, core: 2. Of those that a mesh axis runs over, the one named last changes fastest.
Arguments:
- trial_potential: float32 [2, 128, 64, 128], P(None, 'pw'), may hold values from -6 to 6
- local_potential: float32 [128, 64, 128], P('pw'), may hold values from -0.5 to 0.5
- psi_coef: float32 [131072, 16], P('pw', 'band'), may hold values from -6 to 6
- band_energy: float32 [16], replicated, may hold values from -1 to -0.4
- band_slot: int32 [16], P('band'), may hold values from 0 to 15, each once
- pw_index: int32 [131072], P('pw'), may hold values from 0 to 131071, as said below
Outputs:
- density_response: float32 [2, 128, 64, 128], P('pert', 'pw', 'band')
- intersections: float32 [2, 2], replicated
The draws below stay inside these ranges and needn't reach their ends.
Inputs may be any that keep to these rules, and one draw needn't show every extreme that they name: `pw_index`: entry j of each aligned run of 16384 entries is a cell q * 128 + kz of the line q = (j mod 16384) // 16, with kz below 128; the kz of the 16 entries of one line are distinct. `band_slot`: each band appears in exactly one slot.
All inputs are finite; a program needn't handle non-finite values.
Results may differ from the reference program's by a relative error of at most 0.0001.
Values sent between devices are 32-bit elements; how exact they have to be, the bound alone decides.
No kernel may reach another device: no remote copies, remote signals or barrier semaphores. Data moves between devices by JAX's collectives and lax.ppermute only.
A program may use at most 192 MiB of HBM per device.

```python
import math
import jax
import jax.numpy as jnp
from jax import lax

GX = 128
GY = 64
GZ = 128
NPW_DEV = 16384
ITERS = 3
KYD = 8
NPW = 131072
NBANDS = 16
NPERT = 2
N_PW = 8


def draw_pw_index(key, part):
    key = jax.random.fold_in(key, 7)
    line_count = GX * (GY // N_PW)
    per_line = NPW_DEV // line_count

    def one_line(number):
        line = number % line_count
        chosen = jax.random.permutation(jax.random.fold_in(key, number), GZ)
        return (line * GZ + chosen[:per_line]).astype(jnp.int32)
    numbers = jnp.arange(N_PW * line_count, dtype=jnp.int32)
    return jax.vmap(one_line)(numbers).reshape(-1)


def draw_local_potential(key, part):
    key = jax.random.fold_in(key, 11)
    sign_key = jax.random.fold_in(key, 1)
    size_key = jax.random.fold_in(key, 2)
    upward = jax.random.bernoulli(sign_key, 0.5, (GX, GY, GZ))
    signs = jnp.where(upward, 1.0, -1.0).astype(jnp.float32)
    magnitude = jax.random.uniform(size_key, (GX, GY, GZ), jnp.float32, 0.3, 0.5)
    return signs * magnitude


def steps_of(rng, shape, shards, smallest, top_value):
    factor_of = 1.0
    for position, shards_of in shards:
        heights = jax.random.uniform(jax.random.fold_in(jax.random.fold_in(rng, 6), position), (shards_of,), jnp.float32, smallest / len(shards), top_value / len(shards))
        factor_of = factor_of * jnp.repeat(jnp.exp(heights), shape[position] // shards_of).reshape((-1,) + (1,) * (len(shape) - 1 - position))
    return factor_of


def normal_values(own_key, shape, deviation, limit, pieces=(), kind=jnp.bfloat16):
    result = jax.random.normal(own_key, shape, jnp.float32) * deviation
    if len(pieces) > 0:
        result = steps_of(own_key, shape, pieces, -0.22, 0.18) * result
    return jnp.clip(result, min=-limit, max=limit).astype(kind)


def setup_inputs(seed: int = 0) -> dict:
    keys = jax.random.split(jax.random.key(seed), 7)
    return {
        "trial_potential": normal_values(keys[0], (NPERT, GX, GY, GZ), 1.0, 6.0, ((1, 8),), jnp.float32),
        "local_potential": draw_local_potential(jax.random.fold_in(keys[6], 71), 0),
        "psi_coef": normal_values(keys[2], (NPW, NBANDS), 1.0, 6.0, ((0, 8), (1, 16)), jnp.float32),
        "band_energy": jnp.clip(jax.random.uniform(keys[3], (NBANDS,), jnp.float32, -1.0, -0.4), -1.0, -0.4),
        "band_slot": jax.random.permutation(keys[4], NBANDS).astype(jnp.int32),
        "pw_index": draw_pw_index(jax.random.fold_in(keys[6], 71), 0),
    }


highest = lax.Precision.HIGHEST

def hartley_table(points):
    wave_index = jnp.arange(points, dtype=jnp.int32)
    phase_table = wave_index[:, None] * wave_index[None, :] % points
    angles = phase_table.astype(jnp.float32) * (2.0 * math.pi / points)
    return (jnp.cos(angles) + jnp.sin(angles)) / math.sqrt(points)

def wave_energy(wave_number, points):
    folded = jnp.minimum(wave_number, points - wave_number).astype(jnp.float32)
    return 4.0 * (folded / points) ** 2

def transform3(field, table_x, table_y, table_z):
    field = jnp.einsum('...xyz,xa->...ayz', field, table_x, precision=highest)
    field = jnp.einsum('...xyz,ya->...xaz', field, table_y, precision=highest)
    return jnp.einsum('...xyz,za->...xya', field, table_z, precision=highest)

def reference(trial_potential, local_potential, psi_coef, band_energy, band_slot, pw_index):
    table_x = hartley_table(GX)
    table_y = hartley_table(GY)
    table_z = hartley_table(GZ)
    owner_block = jnp.arange(NPW, dtype=jnp.int32) // NPW_DEV
    wave_x = pw_index // (KYD * GZ)
    wave_y = owner_block * KYD + pw_index // GZ % KYD
    wave_z = pw_index % GZ
    flat_cells = ((wave_x * GY + wave_y) * GZ + wave_z).astype(jnp.int32)
    kinetic = wave_energy(wave_x, GX) + wave_energy(wave_y, GY) + wave_energy(wave_z, GZ)
    energies = band_energy[band_slot]

    def to_grid(coefficients):
        coef_grid = jnp.zeros(coefficients.shape[:-1] + (GX * GY * GZ,), jnp.float32)
        coef_grid = coef_grid.at[..., flat_cells].set(coefficients)
        coef_grid = coef_grid.reshape(coefficients.shape[:-1] + (GX, GY, GZ))
        return transform3(coef_grid, table_x, table_y, table_z)

    def to_coeffs(fields):
        spectrum = transform3(fields, table_x, table_y, table_z)
        return spectrum.reshape(fields.shape[:-3] + (GX * GY * GZ,))[..., flat_cells]

    def project(values):
        intersection = jnp.dot(values, psi_coef, precision=highest)
        return values - jnp.dot(intersection, psi_coef.T, precision=highest) / NPW

    def one_band(density, inputs):
        column, energy = inputs
        psi_grid = to_grid(column)
        driving = -project(to_coeffs(trial_potential * psi_grid))
        inverse_diag = 1.0 / (kinetic - energy)
        response = inverse_diag * driving
        for iteration in range(ITERS):
            applied = kinetic * response + to_coeffs(local_potential * to_grid(response)) - energy * response
            response = response + inverse_diag * (driving - project(applied))
        density = density + 2.0 * psi_grid * to_grid(response)
        return (density, None)
    start = jnp.zeros((NPERT, GX, GY, GZ), jnp.float32)
    density, unused = lax.scan(one_band, start, (psi_coef.T, energies))
    intersections = jnp.einsum('ixyz,jxyz->ij', trial_potential, density, precision=highest) / (NBANDS * NPW)
    return (density, intersections)
```

```python
import math
from functools import partial

import jax
import jax.numpy as jnp
import numpy as np
from jax import lax
from jax.experimental import pallas as pl
from jax.experimental.pallas import tpu as pltpu
from jax.sharding import PartitionSpec as P

ITERS = 3
F32 = jnp.float32
BF16 = jnp.bfloat16
VMEM_LIMIT = 48 * 1024 * 1024


def hartley_pieces(points):
    wave_index = np.arange(points)
    angles = (wave_index[:, None] * wave_index[None, :] % points) * (2.0 * math.pi / points)
    table = (np.cos(angles) + np.sin(angles)) / math.sqrt(points)
    high = table.astype(np.float32).astype(jnp.bfloat16)
    low = (table - high.astype(np.float64)).astype(np.float32).astype(jnp.bfloat16)
    return high, low


def left_table(points):
    high, low = hartley_pieces(points)
    return np.concatenate([high, high, low], axis=1)


def right_table(points):
    high, low = hartley_pieces(points)
    return np.concatenate([high, high, low], axis=0)


def stack_pieces(values, axis):
    high = values.astype(BF16)
    low = (values - high.astype(F32)).astype(BF16)
    return jnp.concatenate([high, low, high], axis=axis)


def from_left(table, values):
    return jnp.dot(table, stack_pieces(values, 0), preferred_element_type=F32)


def from_right(values, table):
    return jnp.dot(stack_pieces(values, 1), table, preferred_element_type=F32)


def pick(values, lanes):
    return jnp.take_along_axis(values, lanes, axis=1, mode="promise_in_bounds")


def lane_numbers(shape):
    return lax.broadcasted_iota(jnp.int32, shape, len(shape) - 1)


class Sizes:
    def __init__(self, size_x, size_y, size_z, parts, per_line):
        self.x, self.y, self.z, self.parts, self.c = size_x, size_y, size_z, parts, per_line
        self.slab_x, self.slab_y = size_x // parts, size_y // parts


def send_lines(s, flat, inverse_ref, table_x, send_ref):
    for ky in range(s.slab_y):
        lanes = inverse_ref[ky]
        placed = jnp.where(lanes >= 0, pick(flat, jnp.maximum(lanes, 0)), 0.0)
        lines = from_left(table_x, placed)
        for part in range(s.parts):
            rows = lines[part * s.slab_x : (part + 1) * s.slab_x]
            send_ref[part, pl.ds(ky, s.slab_x, s.slab_y), :] = rows


def read_lines(s, recv_ref, first_row, depth, table_x):
    result = jnp.zeros((s.x, s.slab_y * s.c), F32)
    group = lane_numbers(result.shape) // s.c
    for ky in range(s.slab_y):
        lines = jnp.concatenate(
            [
                recv_ref[source, pl.ds(first_row + ky, s.slab_x, s.slab_y), :]
                for source in range(s.parts)
            ],
            axis=0,
        )
        values = pick(from_left(table_x, lines), depth)
        result = jnp.where(group == ky, values, result)
    return result


def slab_in(s, recv_ref, rows, table_y):
    lines = recv_ref[:, rows * s.slab_y : (rows + 1) * s.slab_y, :]
    return from_left(table_y, lines.reshape(s.y, s.z))


def slab_out(s, values, table_y, send_ref, first_row, rows):
    lines = from_left(table_y, values).reshape(s.parts, s.slab_y, s.z)
    start = first_row + rows * s.slab_y
    send_ref[:, start : start + s.slab_y, :] = lines


def band_dots(all_bands, flat):
    return jnp.sum(all_bands * flat[None], axis=1)


def band_sum(all_bands, weights):
    total = weights[0:1, :] * all_bands[0]
    for band in range(1, all_bands.shape[0]):
        total = total + weights[band : band + 1, :] * all_bands[band]
    return total


def total_weights(parts, coef_total):
    summed = jnp.sum(jnp.sum(parts, axis=0), axis=1, keepdims=True)
    return jnp.broadcast_to(summed * (1.0 / coef_total), parts.shape[1:])


def wave_energy(wave_number, points):
    folded = jnp.minimum(wave_number, points - wave_number).astype(F32)
    return 4.0 * (folded * (1.0 / points)) ** 2


def start_kernel(s, part_ref, slot_ref, energy_ref, psi_ref, index_ref, tx_ref,
                 send_ref, inverse_ref, depth_ref, diag_ref):
    depth = index_ref[...] % s.z
    depth_ref[...] = depth
    lanes = lane_numbers((s.x, s.z))
    for ky in range(s.slab_y):
        inverse = jnp.full((s.x, s.z), -1, jnp.int32)
        for c in range(s.c):
            lane = ky * s.c + c
            same = pick(depth, jnp.full((s.x, s.z), lane, jnp.int32))
            inverse = jnp.where(same == lanes, lane, inverse)
        inverse_ref[ky] = inverse
    wave_x = lax.broadcasted_iota(jnp.int32, depth.shape, 0)
    wave_y = part_ref[0] * s.slab_y + lane_numbers(depth.shape) // s.c
    kinetic = wave_energy(wave_x, s.x) + wave_energy(wave_y, s.y) + wave_energy(depth, s.z)
    diag_ref[...] = 1.0 / (kinetic - energy_ref[slot_ref[0]])
    send_lines(s, psi_ref[...], inverse_ref, tx_ref[...], send_ref)


def driving_kernel(s, recv_ref, trial_ref, local_ref, tyl_ref, tzr_ref,
                   send_ref, grid_ref):
    table_y, table_z = tyl_ref[...], tzr_ref[...]
    block = s.slab_x * s.slab_y
    group = 4
    for first in range(0, s.slab_x, group):
        inner = jnp.concatenate(
            [slab_in(s, recv_ref, row, table_y) for row in range(first, first + group)], axis=0
        )
        rows = pl.ds(first * s.y, group * s.y)
        grid = from_right(inner, table_z)
        grid_ref[rows, :] = grid
        for number, potential in enumerate((trial_ref[0, rows, :], local_ref[rows, :])):
            outer = from_right(potential * grid, table_z)
            for row in range(group):
                slab_out(s, outer[row * s.y : (row + 1) * s.y], table_y, send_ref,
                         number * block, first + row)


def project_kernel(s, recv_ref, depth_ref, all_ref, tx_ref, driving_ref, local_ref, dots_ref):
    depth, table_x = depth_ref[...], tx_ref[...]
    driving = read_lines(s, recv_ref, 0, depth, table_x)
    driving_ref[...] = driving
    local_ref[...] = read_lines(s, recv_ref, s.slab_x * s.slab_y, depth, table_x)
    dots = band_dots(all_ref[...], driving)
    dots_ref[...] = jnp.broadcast_to(dots[None], dots_ref.shape)


def first_kernel(s, coef_total, dots_ref, driving_ref, all_ref, diag_ref, inverse_ref, tx_ref,
                 send_ref, start_ref):
    weights = total_weights(dots_ref[...], coef_total)
    start = band_sum(all_ref[...], weights) - driving_ref[...]
    start_ref[...] = start
    send_lines(s, start * diag_ref[...], inverse_ref, tx_ref[...], send_ref)


def potential_kernel(s, dots_ref, recv_ref, local_ref, tyl_ref, tzr_ref, send_ref):
    table_y, table_z = tyl_ref[...], tzr_ref[...]
    block = s.slab_x * s.slab_y
    group = 4
    for first in range(0, s.slab_x, group):
        inner = jnp.concatenate(
            [slab_in(s, recv_ref, row, table_y) for row in range(first, first + group)], axis=0
        )
        rows = pl.ds(first * s.y, group * s.y)
        grid = from_right(inner, table_z)
        outer = from_right(local_ref[rows, :] * grid, table_z)
        for row in range(group):
            slab_out(s, outer[row * s.y : (row + 1) * s.y], table_y, send_ref, 0, first + row)
    dots = dots_ref[...]
    send_ref[:, block:, :] = jnp.broadcast_to(dots[None], (s.parts,) + dots.shape)


def dots_kernel(s, all_ref, image_ref, diag_ref, start_ref, dots_ref):
    dots_ref[...] = band_dots(all_ref[...] + diag_ref[...][None] * image_ref[...], start_ref[...])


def update_kernel(s, coef_total, last, recv_ref, start_ref, depth_ref, all_ref, image_ref,
                  diag_ref, inverse_ref, tx_ref, own_ref, other_ref, send_ref, dots_ref=None):
    block = s.slab_x * s.slab_y
    table_x = tx_ref[...]
    weights = total_weights(recv_ref[:, block:, :], coef_total)
    change = read_lines(s, recv_ref, 0, depth_ref[...], table_x)
    all_bands = all_ref[...]
    state = start_ref[...] - change + band_sum(all_bands, weights)
    response = state * diag_ref[...]
    send_lines(s, response, inverse_ref, table_x, send_ref)
    if not last:
        dots_ref[...] = band_dots(all_bands + diag_ref[...][None] * image_ref[...], state)
        return
    own = jnp.sum(own_ref[...] * response, axis=0, keepdims=True)
    other = jnp.sum(other_ref[...] * response, axis=0, keepdims=True)
    sums = jnp.concatenate([own, other, jnp.zeros((6, s.z), F32)], axis=0)
    send_ref[:, block:, :] = jnp.broadcast_to(sums[None], (s.parts,) + sums.shape)


def density_kernel(s, bands, recv_ref, grid_ref, tyl_ref, tzr_ref, send_ref):
    table_y, table_z = tyl_ref[...], tzr_ref[...]
    group = 4
    keep = s.y // bands
    for first in range(0, s.slab_x, group):
        inner = jnp.concatenate(
            [slab_in(s, recv_ref, row, table_y) for row in range(first, first + group)], axis=0
        )
        rows = pl.ds(first * s.y, group * s.y)
        density = 2.0 * grid_ref[rows, :] * from_right(inner, table_z)
        for row in range(group):
            for band in range(bands):
                start = row * s.y + band * keep
                place = (first + row) * keep
                send_ref[band, place : place + keep, :] = density[start : start + keep]
    sums = jnp.sum(recv_ref[:, s.slab_x * s.slab_y :, :], axis=0)
    send_ref[:, s.slab_x * keep :, :] = jnp.broadcast_to(sums[None], (bands,) + sums.shape)


def final_kernel(s, rows, recv_ref, density_ref, sums_ref):
    total = jnp.sum(recv_ref[...], axis=0)
    density_ref[...] = total[:rows]
    lanes = jnp.sum(total[rows:], axis=1, keepdims=True)
    sums_ref[...] = jnp.broadcast_to(lanes, sums_ref.shape)


def call(kernel, out_shape, scalars=0, name=None):
    smem = pl.BlockSpec(memory_space=pltpu.SMEM)
    vmem = pl.BlockSpec(memory_space=pltpu.VMEM)

    def run(*operands):
        return pl.pallas_call(
            kernel,
            out_shape=out_shape,
            in_specs=[smem] * scalars + [vmem] * (len(operands) - scalars),
            out_specs=jax.tree.map(lambda _: vmem, out_shape),
            compiler_params=pltpu.CompilerParams(vmem_limit_bytes=VMEM_LIMIT),
            name=name,
        )(*operands)

    return run


def shape(*sizes, dtype=F32):
    return jax.ShapeDtypeStruct(sizes, dtype)


def per_device(trial_potential, local_potential, psi_coef, band_energy, band_slot, pw_index):
    parts = lax.axis_size("pw")
    band_count = lax.axis_size("band")
    slab_x, size_y, size_z = local_potential.shape
    size_x = slab_x * parts
    coef_count = psi_coef.shape[0]
    coef_total = coef_count * parts
    total_bands = band_energy.shape[0]
    total_perts = trial_potential.shape[0]
    slab_y = size_y // parts
    s = Sizes(size_x, size_y, size_z, parts, coef_count // (size_x * slab_y))
    block = slab_x * slab_y
    flat = (size_x, slab_y * s.c)
    pert = lax.axis_index("pert")
    part = lax.axis_index("pw").reshape(1).astype(jnp.int32)

    table_x = jnp.asarray(left_table(size_x))
    table_y = jnp.asarray(left_table(size_y))
    table_z = jnp.asarray(right_table(size_z))

    def exchange(values):
        return lax.all_to_all(values, "pw", split_axis=0, concat_axis=0, tiled=True)

    psi = psi_coef.reshape(flat)
    all_psi = lax.all_gather(psi, "band", axis=0)
    send, inverse, depth, diag = call(
        partial(start_kernel, s),
        (
            shape(parts, block, size_z),
            shape(slab_y, size_x, size_z, dtype=jnp.int32),
            shape(*flat, dtype=jnp.int32),
            shape(*flat),
        ),
        3,
        "start",
    )(part, band_slot, band_energy, psi, pw_index.reshape(flat), table_x)
    recv = exchange(send)

    local = local_potential.reshape(slab_x * size_y, size_z)
    trials = trial_potential.reshape(total_perts, slab_x * size_y, size_z)
    trial = lax.dynamic_slice_in_dim(trials, pert, 1, 0)
    send, psi_grid = call(
        partial(driving_kernel, s),
        (shape(parts, 2 * block, size_z), shape(slab_x * size_y, size_z)),
        0,
        "driving",
    )(recv, trial, local, table_y, table_z)
    recv = exchange(send)

    driving, image, dots = call(
        partial(project_kernel, s),
        (shape(*flat), shape(*flat), shape(parts, total_bands, size_z)),
        0,
        "project",
    )(recv, depth, all_psi, table_x)
    all_image = lax.all_gather(image, "band", axis=0)
    other = lax.ppermute(driving, "pert", [(0, 1), (1, 0)])
    dots = exchange(dots)
    send, start = call(
        partial(first_kernel, s, coef_total),
        (shape(parts, block, size_z), shape(*flat)),
        0,
        "first",
    )(dots, driving, all_psi, diag, inverse, table_x)
    for iteration in range(ITERS):
        last = iteration == ITERS - 1
        recv = exchange(send)
        if iteration == 0:
            dots = call(partial(dots_kernel, s), shape(total_bands, size_z), 0, "dots")(
                all_psi, all_image, diag, start
            )
        send = call(
            partial(potential_kernel, s),
            shape(parts, block + total_bands, size_z),
            0,
            "potential",
        )(dots, recv, local, table_y, table_z)
        recv = exchange(send)
        if last:
            outs = (shape(parts, block + 8, size_z),)
        else:
            outs = (shape(parts, block, size_z), shape(total_bands, size_z))
        send, *rest = call(partial(update_kernel, s, coef_total, last), outs, 0, "update")(
            recv, start, depth, all_psi, all_image, diag, inverse, table_x, driving, other
        )
        dots = rest[0] if rest else None

    recv = exchange(send)
    rows = slab_x * (size_y // band_count)
    send = call(
        partial(density_kernel, s, band_count),
        shape(band_count, rows + 8, size_z),
        0,
        "density",
    )(recv, psi_grid, table_y, table_z)
    recv = lax.all_to_all(send, "band", split_axis=0, concat_axis=0, tiled=True)
    density, sums = call(
        partial(final_kernel, s, rows), (shape(rows, size_z), shape(8, size_z)), 0, "final"
    )(recv)
    own = sums[:2, 0] * (2.0 / (total_bands * coef_total))
    across = lax.ppermute(own, "pert", [(0, 1), (1, 0)])
    first = jnp.stack([own, across[::-1]], axis=1)
    second = jnp.stack([across, own[::-1]], axis=1)
    intersections = jnp.where(pert == 0, first, second)
    return (
        density.reshape(1, slab_x, size_y // band_count, size_z),
        intersections,
    )


def solution(mesh):
    return jax.shard_map(
        per_device,
        mesh=mesh,
        in_specs=(
            P(None, "pw", None, None),
            P("pw", None, None),
            P("pw", "band"),
            P(),
            P("band"),
            P("pw"),
        ),
        out_specs=(P("pert", "pw", "band", None), P()),
        check_vma=False,
    )
```

```python
import math
from functools import partial

import jax
import jax.numpy as jnp
import numpy as np
from jax import lax
from jax.experimental import pallas as pl
from jax.experimental.pallas import tpu as pltpu
from jax.sharding import PartitionSpec as P

ITERS = 3
F32 = jnp.float32
BF16 = jnp.bfloat16
VMEM_LIMIT = 16 * 1024 * 1024


def hartley_pieces(points):
    wave_index = np.arange(points)
    angles = (wave_index[:, None] * wave_index[None, :] % points) * (2.0 * math.pi / points)
    table = (np.cos(angles) + np.sin(angles)) / math.sqrt(points)
    high = table.astype(np.float32).astype(jnp.bfloat16)
    low = (table - high.astype(np.float64)).astype(np.float32).astype(jnp.bfloat16)
    return high, low


def left_table(points):
    high, low = hartley_pieces(points)
    return np.concatenate([high, high, low], axis=1)


def right_table(points):
    high, low = hartley_pieces(points)
    return np.concatenate([high, high, low], axis=0)


def stack_pieces(values, axis):
    high = values.astype(BF16)
    low = (values - high.astype(F32)).astype(BF16)
    return jnp.concatenate([high, low, high], axis=axis)


def from_left(table, values):
    return jnp.dot(table, stack_pieces(values, 0), preferred_element_type=F32)


def all_from_left(table, blocks):
    results = []
    for first in range(0, len(blocks), 2):
        pair = blocks[first : first + 2]
        width = pair[0].shape[1]
        wide = from_left(table, jnp.concatenate(pair, axis=1))
        results += [wide[:, n * width : (n + 1) * width] for n in range(len(pair))]
    return results


def from_right(values, table):
    return jnp.dot(stack_pieces(values, 1), table, preferred_element_type=F32)


def pick(values, lanes):
    return jnp.take_along_axis(values, lanes, axis=1, mode="promise_in_bounds")


def lane_numbers(shape):
    return lax.broadcasted_iota(jnp.int32, shape, len(shape) - 1)


class Sizes:
    def __init__(self, size_x, size_y, size_z, parts, per_line):
        self.x, self.y, self.z, self.parts, self.c = size_x, size_y, size_z, parts, per_line
        self.slab_x, self.slab_y = size_x // parts, size_y // parts


def send_lines(s, flat, inverse_ref, table_x, send_ref):
    placed = []
    for ky in range(s.slab_y):
        lanes = inverse_ref[ky]
        placed.append(jnp.where(lanes >= 0, pick(flat, jnp.maximum(lanes, 0)), 0.0))
    for ky, lines in enumerate(all_from_left(table_x, placed)):
        for part in range(s.parts):
            rows = lines[part * s.slab_x : (part + 1) * s.slab_x]
            send_ref[part, pl.ds(ky, s.slab_x, s.slab_y), :] = rows


def read_lines(s, recv_ref, depth, table_x):
    result = jnp.zeros((s.x, s.slab_y * s.c), F32)
    group = lane_numbers(result.shape) // s.c
    blocks = [
        jnp.concatenate(
            [
                recv_ref[source, pl.ds(ky, s.slab_x, s.slab_y), :]
                for source in range(s.parts)
            ],
            axis=0,
        )
        for ky in range(s.slab_y)
    ]
    for ky, lines in enumerate(all_from_left(table_x, blocks)):
        result = jnp.where(group == ky, pick(lines, depth), result)
    return result


def slabs_in(s, recv_ref, rows, table_y):
    blocks = [
        recv_ref[:, row * s.slab_y : (row + 1) * s.slab_y, :].reshape(s.y, s.z) for row in rows
    ]
    return jnp.concatenate(all_from_left(table_y, blocks), axis=0)


def slabs_out(s, values, table_y, send_ref, rows):
    blocks = [values[n * s.y : (n + 1) * s.y] for n in range(len(rows))]
    for row, lines in zip(rows, all_from_left(table_y, blocks)):
        start = row * s.slab_y
        send_ref[:, start : start + s.slab_y, :] = lines.reshape(s.parts, s.slab_y, s.z)


def fold(dots):
    half = dots.shape[0] // 2
    middle = dots.shape[1] // 2
    folded = dots + pltpu.roll(dots, middle, 1)
    return jnp.where(lane_numbers((half, dots.shape[1])) < middle, folded[:half], folded[half:])


def band_dots(all_bands, flat):
    sums = [
        jnp.sum(all_bands[band] * flat, axis=0, keepdims=True)
        for band in range(all_bands.shape[0])
    ]
    return jnp.concatenate(sums, axis=0)


def band_sum(all_bands, weights):
    total = weights[0:1, :] * all_bands[0]
    for band in range(1, all_bands.shape[0]):
        total = total + weights[band : band + 1, :] * all_bands[band]
    return total


def total_weights(parts, coef_total):
    summed = jnp.sum(parts, axis=0) * (1.0 / coef_total)
    early = lane_numbers(summed.shape) < summed.shape[1] // 2
    halves = [
        jnp.sum(jnp.where(early, summed, 0.0), axis=1, keepdims=True),
        jnp.sum(jnp.where(early, 0.0, summed), axis=1, keepdims=True),
    ]
    weights = jnp.concatenate(halves, axis=0)
    return jnp.broadcast_to(weights, (weights.shape[0], summed.shape[1]))


def wave_energy(wave_number, points):
    folded = jnp.minimum(wave_number, points - wave_number).astype(F32)
    return 4.0 * (folded * (1.0 / points)) ** 2


def start_kernel(s, part_ref, slot_ref, energy_any, psi_any, index_any, tx_any,
                 send_ref, inverse_ref, depth_ref, diag_ref,
                 energy_ref, psi_ref, index_ref, tx_ref, sems):
    copies = [
        pltpu.make_async_copy(source, target, sems.at[number])
        for number, (source, target) in enumerate(
            ((index_any, index_ref), (energy_any, energy_ref), (psi_any, psi_ref), (tx_any, tx_ref))
        )
    ]
    for copy in copies:
        copy.start()
    for copy in copies:
        copy.wait()
    depth = index_ref[...] % s.z
    depth_ref[...] = depth
    turned = depth.T
    cells = lax.broadcasted_iota(jnp.int32, (s.z, s.x), 0)
    for ky in range(s.slab_y):
        inverse = jnp.full((s.z, s.x), -1, jnp.int32)
        for c in range(s.c):
            lane = ky * s.c + c
            inverse = jnp.where(turned[lane : lane + 1, :] == cells, lane, inverse)
        inverse_ref[ky] = inverse.T
    wave_x = lax.broadcasted_iota(jnp.int32, depth.shape, 0)
    wave_y = part_ref[0] * s.slab_y + lane_numbers(depth.shape) // s.c
    kinetic = wave_energy(wave_x, s.x) + wave_energy(wave_y, s.y) + wave_energy(depth, s.z)
    diag_ref[...] = 1.0 / (kinetic - energy_ref[slot_ref[0]])
    send_lines(s, psi_ref[...], inverse_ref, tx_ref[...], send_ref)


def driving_kernel(s, pert_ref, recv_ref, trial_ref, local_ref, tyl_ref, tzr_ref,
                   image_ref, send_ref, grid_ref):
    table_y, table_z = tyl_ref[...], tzr_ref[...]
    group = 4
    for first in range(0, s.slab_x, group):
        inner = slabs_in(s, recv_ref, range(first, first + group), table_y)
        rows = pl.ds(first * s.y, group * s.y)
        grid = from_right(inner, table_z)
        grid_ref[rows, :] = grid
        for potential, out_ref in (
            (local_ref[rows, :], image_ref),
            (trial_ref[pert_ref[0], rows, :], send_ref),
        ):
            outer = from_right(potential * grid, table_z)
            slabs_out(s, outer, table_y, out_ref, range(first, first + group))


def image_kernel(s, recv_ref, depth_ref, tx_ref, image_ref):
    image_ref[...] = read_lines(s, recv_ref, depth_ref[...], tx_ref[...])


def project_kernel(s, recv_ref, depth_ref, all_ref, tx_ref, driving_ref, dots_ref):
    driving = read_lines(s, recv_ref, depth_ref[...], tx_ref[...])
    driving_ref[...] = driving
    dots = fold(band_dots(all_ref, driving))
    dots_ref[...] = jnp.broadcast_to(dots[None], dots_ref.shape)


def first_kernel(s, coef_total, dots_ref, driving_ref, all_ref, diag_ref, inverse_ref,
                 tx_ref, send_ref, start_ref):
    weights = total_weights(dots_ref[...], coef_total)
    start = band_sum(all_ref, weights) - driving_ref[...]
    start_ref[...] = start
    send_lines(s, start * diag_ref[...], inverse_ref, tx_ref[...], send_ref)


def potential_kernel(s, dots_ref, *refs):
    apply_potential(s, dots_ref[...], *refs)


def apply_potential(s, dots, recv_ref, local_ref, tyl_ref, tzr_ref, send_ref):
    table_y, table_z = tyl_ref[...], tzr_ref[...]
    block = s.slab_x * s.slab_y
    group = 4
    for first in range(0, s.slab_x, group):
        inner = slabs_in(s, recv_ref, range(first, first + group), table_y)
        rows = pl.ds(first * s.y, group * s.y)
        grid = from_right(inner, table_z)
        outer = from_right(local_ref[rows, :] * grid, table_z)
        slabs_out(s, outer, table_y, send_ref, range(first, first + group))
    send_ref[:, block:, :] = jnp.broadcast_to(dots[None], (s.parts,) + dots.shape)


def state_dots(bands, images, diag, state):
    return fold(band_dots(bands, state) + band_dots(images, diag * state))


def first_potential_kernel(s, other_ref, all_ref, image_ref, diag_ref, start_ref, *refs):
    dots = state_dots(all_ref, image_ref, diag_ref[...], start_ref[...])
    apply_potential(s, dots, *refs)


def update_kernel(s, coef_total, last, pert_ref, recv_ref, start_ref, depth_ref, all_ref,
                  image_ref, diag_ref, inverse_ref, tx_ref, own_ref, other_ref, send_ref, dots_ref=None):
    block = s.slab_x * s.slab_y
    table_x = tx_ref[...]
    weights = total_weights(recv_ref[:, block:, :], coef_total)
    change = read_lines(s, recv_ref, depth_ref[...], table_x)
    diag = diag_ref[...]
    state = start_ref[...] - change + band_sum(all_ref, weights)
    response = state * diag
    send_lines(s, response, inverse_ref, table_x, send_ref)
    if not last:
        dots_ref[...] = state_dots(all_ref, image_ref, diag, state)
        return
    own = jnp.sum(own_ref[...] * response, axis=0, keepdims=True)
    other = jnp.sum(other_ref[...] * response, axis=0, keepdims=True)
    lead = pert_ref[0] == 0
    rest = jnp.zeros((6, own.shape[1]), F32)
    sums = jnp.concatenate(
        [jnp.where(lead, own, other), jnp.where(lead, other, own), rest], axis=0
    )
    send_ref[:, block:, :] = jnp.broadcast_to(sums[None], (s.parts,) + sums.shape)


def density_kernel(s, bands, core_ref, recv_ref, grid_ref, tyl_ref, tzr_ref, send_ref):
    table_y, table_z = tyl_ref[...], tzr_ref[...]
    group = 4
    keep = s.y // bands
    for first in range(0, s.slab_x, group):
        inner = slabs_in(s, recv_ref, range(first, first + group), table_y)
        rows = pl.ds(first * s.y, group * s.y)
        density = 2.0 * grid_ref[rows, :] * from_right(inner, table_z)
        for row in range(group):
            for band in range(bands):
                start = row * s.y + band * keep
                place = (first + row) * keep
                slot = core_ref[0] if band % 2 == 0 else 1 - core_ref[0]
                send_ref[slot, band // 2, place : place + keep, :] = density[start : start + keep]
    sums = jnp.sum(recv_ref[:, s.slab_x * s.slab_y :, :], axis=0)
    send_ref[:, :, s.slab_x * keep :, :] = jnp.broadcast_to(
        sums[None, None], (2, bands // 2) + sums.shape
    )


def final_kernel(s, rows, recv_ref, density_ref, sums_ref):
    total = jnp.sum(recv_ref[...], axis=0)
    density_ref[...] = total[:rows]
    lanes = jnp.sum(total[rows:], axis=1, keepdims=True)
    sums_ref[...] = jnp.broadcast_to(lanes, sums_ref.shape)


def call(kernel, out_shape, scalars=0, name=None):
    smem = pl.BlockSpec(memory_space=pltpu.SMEM)
    vmem = pl.BlockSpec(memory_space=pltpu.VMEM)

    def run(*operands):
        return pl.pallas_call(
            kernel,
            out_shape=out_shape,
            in_specs=[smem] * scalars + [vmem] * (len(operands) - scalars),
            out_specs=jax.tree.map(lambda _: vmem, out_shape),
            compiler_params=pltpu.CompilerParams(vmem_limit_bytes=VMEM_LIMIT),
            name=name,
        )(*operands)

    return run


def shape(*sizes, dtype=F32):
    return jax.ShapeDtypeStruct(sizes, dtype)


def per_device(trial_potential, local_potential, psi_coef, band_energy, band_slot, pw_index):
    parts = lax.axis_size("pw")
    band_count = lax.axis_size("band")
    slab_x, size_y, size_z = local_potential.shape
    size_x = slab_x * parts
    coef_count = psi_coef.shape[0]
    coef_total = coef_count * parts
    total_bands = band_energy.shape[0]
    total_perts = trial_potential.shape[0]
    slab_y = size_y // parts
    s = Sizes(size_x, size_y, size_z, parts, coef_count // (size_x * slab_y))
    block = slab_x * slab_y
    flat = (size_x, slab_y * s.c)
    pert = lax.axis_index("pert").astype(jnp.int32)
    part = lax.axis_index("pw").astype(jnp.int32)
    core = lax.axis_index("band").astype(jnp.int32) & 1
    own_column = lax.broadcasted_iota(jnp.int32, (total_perts, total_perts), 1) == pert
    part, pert, core, own_column, slot = lax.optimization_barrier(
        (part.reshape(1), pert.reshape(1), core.reshape(1), own_column, band_slot)
    )

    table_x = jnp.asarray(left_table(size_x))
    table_y = jnp.asarray(left_table(size_y))
    table_z = jnp.asarray(right_table(size_z))

    def exchange(values):
        return lax.all_to_all(values, "pw", split_axis=0, concat_axis=0, tiled=True)

    psi = psi_coef.reshape(flat)
    index = pw_index.reshape(flat)
    all_psi = lax.all_gather(psi, "band", axis=0)
    anywhere = pl.BlockSpec(memory_space=pltpu.HBM)
    smem = pl.BlockSpec(memory_space=pltpu.SMEM)
    vmem = pl.BlockSpec(memory_space=pltpu.VMEM)
    send, inverse, depth, diag = pl.pallas_call(
        partial(start_kernel, s),
        out_shape=(
            shape(parts, block, size_z),
            shape(slab_y, size_x, size_z, dtype=jnp.int32),
            shape(*flat, dtype=jnp.int32),
            shape(*flat),
        ),
        in_specs=[smem, smem] + [anywhere] * 4,
        out_specs=(vmem,) * 4,
        scratch_shapes=[
            pltpu.SMEM(band_energy.shape, F32),
            pltpu.VMEM(flat, F32),
            pltpu.VMEM(flat, jnp.int32),
            pltpu.VMEM(table_x.shape, BF16),
            pltpu.SemaphoreType.DMA((4,)),
        ],
        compiler_params=pltpu.CompilerParams(vmem_limit_bytes=VMEM_LIMIT),
        name="start",
    )(part, slot, band_energy, psi, index, table_x)
    recv = exchange(send)

    local = local_potential.reshape(slab_x * size_y, size_z)
    trials = trial_potential.reshape(total_perts, slab_x * size_y, size_z)
    image_send, send, psi_grid = call(
        partial(driving_kernel, s),
        (
            shape(parts, block, size_z),
            shape(parts, block, size_z),
            shape(slab_x * size_y, size_z),
        ),
        1,
        "driving",
    )(pert, recv, trials, local, table_y, table_z)
    recv = exchange(image_send)
    image = call(partial(image_kernel, s), shape(*flat), 0, "image")(recv, depth, table_x)
    all_image = lax.all_gather(image, "band", axis=0)
    send, _, all_psi = lax.optimization_barrier((send, image, all_psi))
    recv = exchange(send)
    driving, dots = call(
        partial(project_kernel, s),
        (shape(*flat), shape(parts, total_bands // 2, size_z)),
        0,
        "project",
    )(recv, depth, all_psi, table_x)
    dots = exchange(dots)
    send, start = call(
        partial(first_kernel, s, coef_total),
        (shape(parts, block, size_z), shape(*flat)),
        0,
        "first",
    )(dots, driving, all_psi, diag, inverse, table_x)
    other = lax.ppermute(driving, "pert", [(0, 1), (1, 0)])
    for iteration in range(ITERS):
        last = iteration == ITERS - 1
        recv = exchange(send)
        out = shape(parts, block + total_bands // 2, size_z)
        if iteration == 0:
            send = call(partial(first_potential_kernel, s), out, 0, "potential")(
                other, all_psi, all_image, diag, start, recv, local, table_y, table_z
            )
        else:
            send = call(partial(potential_kernel, s), out, 0, "potential")(
                dots, recv, local, table_y, table_z
            )
        recv = exchange(send)
        if last:
            outs = (shape(parts, block + 8, size_z),)
        else:
            outs = (shape(parts, block, size_z), shape(total_bands // 2, size_z))
        send, *rest = call(partial(update_kernel, s, coef_total, last), outs, 1, "update")(
            pert, recv, start, depth, all_psi, all_image, diag, inverse, table_x, driving,
            other,
        )
        dots = rest[0] if rest else None

    recv = exchange(send)
    rows = slab_x * (size_y // band_count)
    send = call(
        partial(density_kernel, s, band_count),
        shape(2, band_count // 2, rows + 8, size_z),
        1,
        "density",
    )(core, recv, psi_grid, table_y, table_z)
    got = lax.ppermute(send[1], "band", [(band, band ^ 1) for band in range(band_count)])
    near = [[2 * z + c for z in range(band_count // 2)] for c in range(2)]
    recv = lax.all_to_all(
        send[0] + got, "band", split_axis=0, concat_axis=0, tiled=True, axis_index_groups=near
    )
    density, sums = call(
        partial(final_kernel, s, rows), (shape(rows, size_z), shape(8, size_z)), 0, "final"
    )(recv)
    own = sums[:total_perts, :total_perts] * (2.0 / (total_bands * coef_total))
    across = lax.ppermute(own, "pert", [(0, 1), (1, 0)])
    intersections = jnp.where(own_column, own, across)
    return (
        density.reshape(1, slab_x, size_y // band_count, size_z),
        intersections,
    )


def solution(mesh):
    return jax.shard_map(
        per_device,
        mesh=mesh,
        in_specs=(
            P(None, "pw", None, None),
            P("pw", None, None),
            P("pw", "band"),
            P(),
            P("band"),
            P("pw"),
        ),
        out_specs=(P("pert", "pw", "band", None), P()),
        check_vma=False,
    )
```

```python
import math
from functools import partial

import jax
import jax.numpy as jnp
import numpy as np
from jax import lax
from jax.experimental import pallas as pl
from jax.experimental.pallas import tpu as pltpu
from jax.sharding import PartitionSpec as P

ITERS = 3
F32 = jnp.float32
BF16 = jnp.bfloat16
GROUP = 16
VMEM_LIMIT = 16 * 1024 * 1024


def hartley_pieces(points):
    wave_index = np.arange(points)
    angles = (wave_index[:, None] * wave_index[None, :] % points) * (2.0 * math.pi / points)
    table = (np.cos(angles) + np.sin(angles)) / math.sqrt(points)
    high = table.astype(np.float32).astype(jnp.bfloat16)
    low = (table - high.astype(np.float64)).astype(np.float32).astype(jnp.bfloat16)
    return high, low


def left_table(points):
    high, low = hartley_pieces(points)
    return np.concatenate([high, high, low], axis=1)


def right_table(points):
    high, low = hartley_pieces(points)
    return np.concatenate([high, high, low], axis=0)


def stack_pieces(values, axis):
    high = values.astype(BF16)
    low = (values - high.astype(F32)).astype(BF16)
    return jnp.concatenate([high, low, high], axis=axis)


def from_left(table, values):
    return jnp.dot(table, stack_pieces(values, 0), preferred_element_type=F32)


def all_from_left(table, blocks):
    results = []
    for first in range(0, len(blocks), 2):
        pair = blocks[first : first + 2]
        width = pair[0].shape[1]
        wide = from_left(table, jnp.concatenate(pair, axis=1))
        results += [wide[:, n * width : (n + 1) * width] for n in range(len(pair))]
    return results


def from_right(values, table):
    return jnp.dot(stack_pieces(values, 1), table, preferred_element_type=F32)


def pick(values, lanes):
    return jnp.take_along_axis(values, lanes, axis=1, mode="promise_in_bounds")


def lane_numbers(shape):
    return lax.broadcasted_iota(jnp.int32, shape, len(shape) - 1)


class Sizes:
    def __init__(self, size_x, size_y, size_z, parts, per_line):
        self.x, self.y, self.z, self.parts, self.c = size_x, size_y, size_z, parts, per_line
        self.slab_x, self.slab_y = size_x // parts, size_y // parts


def send_lines(s, flat, inverse_ref, table_x, send_ref):
    placed = []
    for ky in range(s.slab_y):
        lanes = inverse_ref[ky]
        placed.append(jnp.where(lanes >= 0, pick(flat, jnp.maximum(lanes, 0)), 0.0))
    for ky, lines in enumerate(all_from_left(table_x, placed)):
        for part in range(s.parts):
            rows = lines[part * s.slab_x : (part + 1) * s.slab_x]
            send_ref[part, pl.ds(ky, s.slab_x, s.slab_y), :] = rows


def read_lines(s, recv_ref, depth, table_x):
    result = jnp.zeros((s.x, s.slab_y * s.c), F32)
    group = lane_numbers(result.shape) // s.c
    blocks = [
        jnp.concatenate(
            [
                recv_ref[source, pl.ds(ky, s.slab_x, s.slab_y), :]
                for source in range(s.parts)
            ],
            axis=0,
        )
        for ky in range(s.slab_y)
    ]
    for ky, lines in enumerate(all_from_left(table_x, blocks)):
        result = jnp.where(group == ky, pick(lines, depth), result)
    return result


def slabs_in(s, recv_ref, rows, table_y):
    blocks = [
        recv_ref[:, row * s.slab_y : (row + 1) * s.slab_y, :].reshape(s.y, s.z) for row in rows
    ]
    return jnp.concatenate(all_from_left(table_y, blocks), axis=0)


def slabs_out(s, values, table_y, send_ref, rows):
    blocks = [values[n * s.y : (n + 1) * s.y] for n in range(len(rows))]
    for row, lines in zip(rows, all_from_left(table_y, blocks)):
        start = row * s.slab_y
        send_ref[:, start : start + s.slab_y, :] = lines.reshape(s.parts, s.slab_y, s.z)


def fold(dots):
    half = dots.shape[0] // 2
    middle = dots.shape[1] // 2
    folded = dots + pltpu.roll(dots, middle, 1)
    return jnp.where(lane_numbers((half, dots.shape[1])) < middle, folded[:half], folded[half:])


def band_dots(all_bands, flat):
    sums = [
        jnp.sum(all_bands[band] * flat, axis=0, keepdims=True)
        for band in range(all_bands.shape[0])
    ]
    return jnp.concatenate(sums, axis=0)


def band_sum(all_bands, weights):
    total = weights[0:1, :] * all_bands[0]
    for band in range(1, all_bands.shape[0]):
        total = total + weights[band : band + 1, :] * all_bands[band]
    return total


def total_weights(parts, coef_total):
    summed = jnp.sum(parts, axis=0) * (1.0 / coef_total)
    early = lane_numbers(summed.shape) < summed.shape[1] // 2
    halves = [
        jnp.sum(jnp.where(early, summed, 0.0), axis=1, keepdims=True),
        jnp.sum(jnp.where(early, 0.0, summed), axis=1, keepdims=True),
    ]
    weights = jnp.concatenate(halves, axis=0)
    return jnp.broadcast_to(weights, (weights.shape[0], summed.shape[1]))


def wave_energy(wave_number, points):
    folded = jnp.minimum(wave_number, points - wave_number).astype(F32)
    return 4.0 * (folded * (1.0 / points)) ** 2


def start_kernel(s, part_ref, slot_ref, energy_any, psi_any, index_any, tx_any,
                 send_ref, inverse_ref, depth_ref, diag_ref,
                 energy_ref, psi_ref, index_ref, tx_ref, sems):
    copies = [
        pltpu.make_async_copy(source, target, sems.at[number])
        for number, (source, target) in enumerate(
            ((index_any, index_ref), (energy_any, energy_ref), (psi_any, psi_ref), (tx_any, tx_ref))
        )
    ]
    for copy in copies:
        copy.start()
    for copy in copies:
        copy.wait()
    depth = index_ref[...] % s.z
    depth_ref[...] = depth
    turned = depth.T
    cells = lax.broadcasted_iota(jnp.int32, (s.z, s.x), 0)
    for ky in range(s.slab_y):
        inverse = jnp.full((s.z, s.x), -1, jnp.int32)
        for c in range(s.c):
            lane = ky * s.c + c
            inverse = jnp.where(turned[lane : lane + 1, :] == cells, lane, inverse)
        inverse_ref[ky] = inverse.T
    wave_x = lax.broadcasted_iota(jnp.int32, depth.shape, 0)
    wave_y = part_ref[0] * s.slab_y + lane_numbers(depth.shape) // s.c
    kinetic = wave_energy(wave_x, s.x) + wave_energy(wave_y, s.y) + wave_energy(depth, s.z)
    diag_ref[...] = 1.0 / (kinetic - energy_ref[slot_ref[0]])
    send_lines(s, psi_ref[...], inverse_ref, tx_ref[...], send_ref)


def band_kernel(s, recv_ref, local_ref, tyl_ref, tzr_ref, image_ref, grid_ref):
    table_y, table_z = tyl_ref[...], tzr_ref[...]
    group = min(s.slab_x, GROUP)
    for first in range(0, s.slab_x, group):
        inner = slabs_in(s, recv_ref, range(first, first + group), table_y)
        rows = pl.ds(first * s.y, group * s.y)
        grid = from_right(inner, table_z)
        grid_ref[rows, :] = grid
        outer = from_right(local_ref[rows, :] * grid, table_z)
        slabs_out(s, outer, table_y, image_ref, range(first, first + group))


def driving_kernel(s, pert_ref, grid_ref, trial_ref, tyl_ref, tzr_ref, send_ref):
    table_y, table_z = tyl_ref[...], tzr_ref[...]
    group = min(s.slab_x, GROUP)
    for first in range(0, s.slab_x, group):
        rows = pl.ds(first * s.y, group * s.y)
        outer = from_right(trial_ref[pert_ref[0], rows, :] * grid_ref[rows, :], table_z)
        slabs_out(s, outer, table_y, send_ref, range(first, first + group))


def image_kernel(s, recv_ref, depth_ref, tx_ref, image_ref):
    image_ref[...] = read_lines(s, recv_ref, depth_ref[...], tx_ref[...])


def project_kernel(s, recv_ref, depth_ref, all_ref, tx_ref, driving_ref, dots_ref):
    driving = read_lines(s, recv_ref, depth_ref[...], tx_ref[...])
    driving_ref[...] = driving
    dots = fold(band_dots(all_ref, driving))
    dots_ref[...] = jnp.broadcast_to(dots[None], dots_ref.shape)


def first_kernel(s, coef_total, dots_ref, driving_ref, all_ref, diag_ref, inverse_ref,
                 tx_ref, send_ref, start_ref):
    weights = total_weights(dots_ref[...], coef_total)
    start = band_sum(all_ref, weights) - driving_ref[...]
    start_ref[...] = start
    send_lines(s, start * diag_ref[...], inverse_ref, tx_ref[...], send_ref)


def potential_kernel(s, dots_ref, *refs):
    apply_potential(s, dots_ref[...], *refs)


def apply_potential(s, dots, recv_ref, local_ref, tyl_ref, tzr_ref, send_ref):
    table_y, table_z = tyl_ref[...], tzr_ref[...]
    block = s.slab_x * s.slab_y
    group = min(s.slab_x, GROUP)
    for first in range(0, s.slab_x, group):
        inner = slabs_in(s, recv_ref, range(first, first + group), table_y)
        rows = pl.ds(first * s.y, group * s.y)
        grid = from_right(inner, table_z)
        outer = from_right(local_ref[rows, :] * grid, table_z)
        slabs_out(s, outer, table_y, send_ref, range(first, first + group))
    send_ref[:, block:, :] = jnp.broadcast_to(dots[None], (s.parts,) + dots.shape)


def state_dots(bands, images, diag, state):
    return fold(band_dots(bands, state) + band_dots(images, diag * state))


def first_potential_kernel(s, other_ref, all_ref, image_ref, diag_ref, start_ref, *refs):
    dots = state_dots(all_ref, image_ref, diag_ref[...], start_ref[...])
    apply_potential(s, dots, *refs)


def update_kernel(s, coef_total, last, pert_ref, recv_ref, start_ref, depth_ref, all_ref,
                  image_ref, diag_ref, inverse_ref, tx_ref, own_ref, other_ref, send_ref, dots_ref=None):
    block = s.slab_x * s.slab_y
    table_x = tx_ref[...]
    weights = total_weights(recv_ref[:, block:, :], coef_total)
    change = read_lines(s, recv_ref, depth_ref[...], table_x)
    diag = diag_ref[...]
    state = start_ref[...] - change + band_sum(all_ref, weights)
    response = state * diag
    send_lines(s, response, inverse_ref, table_x, send_ref)
    if not last:
        dots_ref[...] = state_dots(all_ref, image_ref, diag, state)
        return
    own = jnp.sum(own_ref[...] * response, axis=0, keepdims=True)
    other = jnp.sum(other_ref[...] * response, axis=0, keepdims=True)
    lead = pert_ref[0] == 0
    rest = jnp.zeros((6, own.shape[1]), F32)
    sums = jnp.concatenate(
        [jnp.where(lead, own, other), jnp.where(lead, other, own), rest], axis=0
    )
    send_ref[:, block:, :] = jnp.broadcast_to(sums[None], (s.parts,) + sums.shape)


def density_kernel(s, bands, core_ref, recv_ref, grid_ref, tyl_ref, tzr_ref, send_ref):
    table_y, table_z = tyl_ref[...], tzr_ref[...]
    group = min(s.slab_x, GROUP)
    keep = s.y // bands
    for first in range(0, s.slab_x, group):
        inner = slabs_in(s, recv_ref, range(first, first + group), table_y)
        rows = pl.ds(first * s.y, group * s.y)
        density = 2.0 * grid_ref[rows, :] * from_right(inner, table_z)
        for row in range(group):
            for band in range(bands):
                start = row * s.y + band * keep
                place = (first + row) * keep
                slot = core_ref[0] if band % 2 == 0 else 1 - core_ref[0]
                send_ref[slot, band // 2, place : place + keep, :] = density[start : start + keep]
    sums = jnp.sum(recv_ref[:, s.slab_x * s.slab_y :, :], axis=0)
    send_ref[:, :, s.slab_x * keep :, :] = jnp.broadcast_to(
        sums[None, None], (2, bands // 2) + sums.shape
    )


def final_kernel(s, rows, recv_ref, density_ref, sums_ref):
    total = jnp.sum(recv_ref[...], axis=0)
    density_ref[...] = total[:rows]
    lanes = jnp.sum(total[rows:], axis=1, keepdims=True)
    sums_ref[...] = jnp.broadcast_to(lanes, sums_ref.shape)


def call(kernel, out_shape, scalars=0, name=None):
    smem = pl.BlockSpec(memory_space=pltpu.SMEM)
    vmem = pl.BlockSpec(memory_space=pltpu.VMEM)

    def run(*operands):
        return pl.pallas_call(
            kernel,
            out_shape=out_shape,
            in_specs=[smem] * scalars + [vmem] * (len(operands) - scalars),
            out_specs=jax.tree.map(lambda _: vmem, out_shape),
            compiler_params=pltpu.CompilerParams(vmem_limit_bytes=VMEM_LIMIT),
            name=name,
        )(*operands)

    return run


def shape(*sizes, dtype=F32):
    return jax.ShapeDtypeStruct(sizes, dtype)


def per_device(trial_potential, local_potential, psi_coef, band_energy, band_slot, pw_index):
    parts = lax.axis_size("pw")
    band_count = lax.axis_size("band")
    slab_x, size_y, size_z = local_potential.shape
    size_x = slab_x * parts
    coef_count = psi_coef.shape[0]
    coef_total = coef_count * parts
    total_bands = band_energy.shape[0]
    total_perts = trial_potential.shape[0]
    slab_y = size_y // parts
    s = Sizes(size_x, size_y, size_z, parts, coef_count // (size_x * slab_y))
    block = slab_x * slab_y
    flat = (size_x, slab_y * s.c)
    pert = lax.axis_index("pert").astype(jnp.int32)
    part = lax.axis_index("pw").astype(jnp.int32)
    core = lax.axis_index("band").astype(jnp.int32) & 1
    own_column = lax.broadcasted_iota(jnp.int32, (total_perts, total_perts), 1) == pert
    part, pert, core, own_column, slot = lax.optimization_barrier(
        (part.reshape(1), pert.reshape(1), core.reshape(1), own_column, band_slot)
    )

    table_x = jnp.asarray(left_table(size_x))
    table_y = jnp.asarray(left_table(size_y))
    table_z = jnp.asarray(right_table(size_z))

    def exchange(values):
        return lax.all_to_all(values, "pw", split_axis=0, concat_axis=0, tiled=True)

    psi = psi_coef.reshape(flat)
    index = pw_index.reshape(flat)
    all_psi = lax.all_gather(psi, "band", axis=0)
    anywhere = pl.BlockSpec(memory_space=pltpu.HBM)
    smem = pl.BlockSpec(memory_space=pltpu.SMEM)
    vmem = pl.BlockSpec(memory_space=pltpu.VMEM)
    send, inverse, depth, diag = pl.pallas_call(
        partial(start_kernel, s),
        out_shape=(
            shape(parts, block, size_z),
            shape(slab_y, size_x, size_z, dtype=jnp.int32),
            shape(*flat, dtype=jnp.int32),
            shape(*flat),
        ),
        in_specs=[smem, smem] + [anywhere] * 4,
        out_specs=(vmem,) * 4,
        scratch_shapes=[
            pltpu.SMEM(band_energy.shape, F32),
            pltpu.VMEM(flat, F32),
            pltpu.VMEM(flat, jnp.int32),
            pltpu.VMEM(table_x.shape, BF16),
            pltpu.SemaphoreType.DMA((4,)),
        ],
        compiler_params=pltpu.CompilerParams(vmem_limit_bytes=VMEM_LIMIT),
        name="start",
    )(part, slot, band_energy, psi, index, table_x)
    recv = exchange(send)

    local = local_potential.reshape(slab_x * size_y, size_z)
    trials = trial_potential.reshape(total_perts, slab_x * size_y, size_z)
    send, psi_grid = call(
        partial(band_kernel, s),
        (shape(parts, block, size_z), shape(slab_x * size_y, size_z)),
        0,
        "band",
    )(recv, local, table_y, table_z)
    recv = exchange(send)
    image = call(partial(image_kernel, s), shape(*flat), 0, "image")(recv, depth, table_x)
    all_image = lax.all_gather(image, "band", axis=0)
    psi_grid, image = lax.optimization_barrier((psi_grid, image))
    send = call(partial(driving_kernel, s), shape(parts, block, size_z), 1, "driving")(
        pert, psi_grid, trials, table_y, table_z
    )
    recv = exchange(send)
    driving, dots = call(
        partial(project_kernel, s),
        (shape(*flat), shape(parts, total_bands // 2, size_z)),
        0,
        "project",
    )(recv, depth, all_psi, table_x)
    dots = exchange(dots)
    send, start = call(
        partial(first_kernel, s, coef_total),
        (shape(parts, block, size_z), shape(*flat)),
        0,
        "first",
    )(dots, driving, all_psi, diag, inverse, table_x)
    other = lax.ppermute(driving, "pert", [(0, 1), (1, 0)])
    for iteration in range(ITERS):
        last = iteration == ITERS - 1
        recv = exchange(send)
        out = shape(parts, block + total_bands // 2, size_z)
        if iteration == 0:
            send = call(partial(first_potential_kernel, s), out, 0, "potential")(
                other, all_psi, all_image, diag, start, recv, local, table_y, table_z
            )
        else:
            send = call(partial(potential_kernel, s), out, 0, "potential")(
                dots, recv, local, table_y, table_z
            )
        recv = exchange(send)
        if last:
            outs = (shape(parts, block + 8, size_z),)
        else:
            outs = (shape(parts, block, size_z), shape(total_bands // 2, size_z))
        send, *rest = call(partial(update_kernel, s, coef_total, last), outs, 1, "update")(
            pert, recv, start, depth, all_psi, all_image, diag, inverse, table_x, driving,
            other,
        )
        dots = rest[0] if rest else None

    recv = exchange(send)
    rows = slab_x * (size_y // band_count)
    send = call(
        partial(density_kernel, s, band_count),
        shape(2, band_count // 2, rows + 8, size_z),
        1,
        "density",
    )(core, recv, psi_grid, table_y, table_z)
    got = lax.ppermute(send[1], "band", [(band, band ^ 1) for band in range(band_count)])
    near = [[2 * z + c for z in range(band_count // 2)] for c in range(2)]
    recv = lax.all_to_all(
        send[0] + got, "band", split_axis=0, concat_axis=0, tiled=True, axis_index_groups=near
    )
    density, sums = call(
        partial(final_kernel, s, rows), (shape(rows, size_z), shape(8, size_z)), 0, "final"
    )(recv)
    own = sums[:total_perts, :total_perts] * (2.0 / (total_bands * coef_total))
    across = lax.ppermute(own, "pert", [(0, 1), (1, 0)])
    intersections = jnp.where(own_column, own, across)
    return (
        density.reshape(1, slab_x, size_y // band_count, size_z),
        intersections,
    )


def solution(mesh):
    return jax.shard_map(
        per_device,
        mesh=mesh,
        in_specs=(
            P(None, "pw", None, None),
            P("pw", None, None),
            P("pw", "band"),
            P(),
            P("band"),
            P("pw"),
        ),
        out_specs=(P("pert", "pw", "band", None), P()),
        check_vma=False,
    )
```

```python
import math
from functools import partial

import jax
import jax.numpy as jnp
import numpy as np
from jax import lax
from jax.experimental import pallas as pl
from jax.experimental.pallas import tpu as pltpu
from jax.sharding import PartitionSpec as P

ITERS = 3
F32 = jnp.float32
BF16 = jnp.bfloat16
GROUP = 16
VMEM_LIMIT = 16 * 1024 * 1024


def hartley_pieces(points):
    wave_index = np.arange(points)
    angles = (wave_index[:, None] * wave_index[None, :] % points) * (2.0 * math.pi / points)
    table = (np.cos(angles) + np.sin(angles)) / math.sqrt(points)
    high = table.astype(np.float32).astype(jnp.bfloat16)
    low = (table - high.astype(np.float64)).astype(np.float32).astype(jnp.bfloat16)
    return high, low


def left_table(points):
    high, low = hartley_pieces(points)
    return np.concatenate([high, high, low], axis=1)


def right_table(points):
    high, low = hartley_pieces(points)
    return np.concatenate([high, high, low], axis=0)


def stack_pieces(values, axis):
    high = values.astype(BF16)
    low = (values - high.astype(F32)).astype(BF16)
    return jnp.concatenate([high, low, high], axis=axis)


def from_left(table, values):
    return jnp.dot(table, stack_pieces(values, 0), preferred_element_type=F32)


def all_from_left(table, blocks):
    results = []
    for first in range(0, len(blocks), 2):
        pair = blocks[first : first + 2]
        width = pair[0].shape[1]
        wide = from_left(table, jnp.concatenate(pair, axis=1))
        results += [wide[:, n * width : (n + 1) * width] for n in range(len(pair))]
    return results


def from_right(values, table):
    return jnp.dot(stack_pieces(values, 1), table, preferred_element_type=F32)


def pick(values, lanes):
    return jnp.take_along_axis(values, lanes, axis=1, mode="promise_in_bounds")


def lane_numbers(shape):
    return lax.broadcasted_iota(jnp.int32, shape, len(shape) - 1)


class Sizes:
    def __init__(self, size_x, size_y, size_z, parts, per_line):
        self.x, self.y, self.z, self.parts, self.c = size_x, size_y, size_z, parts, per_line
        self.slab_x, self.slab_y = size_x // parts, size_y // parts


def send_lines(s, flat, inverse_ref, table_x, send_ref):
    placed = []
    for ky in range(s.slab_y):
        lanes = inverse_ref[ky]
        placed.append(jnp.where(lanes >= 0, pick(flat, jnp.maximum(lanes, 0)), 0.0))
    for ky, lines in enumerate(all_from_left(table_x, placed)):
        for part in range(s.parts):
            rows = lines[part * s.slab_x : (part + 1) * s.slab_x]
            send_ref[part, pl.ds(ky, s.slab_x, s.slab_y), :] = rows


def read_lines(s, recv_ref, depth, table_x):
    result = jnp.zeros((s.x, s.slab_y * s.c), F32)
    group = lane_numbers(result.shape) // s.c
    blocks = [
        jnp.concatenate(
            [
                recv_ref[source, pl.ds(ky, s.slab_x, s.slab_y), :]
                for source in range(s.parts)
            ],
            axis=0,
        )
        for ky in range(s.slab_y)
    ]
    for ky, lines in enumerate(all_from_left(table_x, blocks)):
        result = jnp.where(group == ky, pick(lines, depth), result)
    return result


def slabs_in(s, recv_ref, rows, table_y):
    blocks = [
        recv_ref[:, row * s.slab_y : (row + 1) * s.slab_y, :].reshape(s.y, s.z) for row in rows
    ]
    return jnp.concatenate(all_from_left(table_y, blocks), axis=0)


def slabs_out(s, values, table_y, send_ref, rows):
    blocks = [values[n * s.y : (n + 1) * s.y] for n in range(len(rows))]
    for row, lines in zip(rows, all_from_left(table_y, blocks)):
        start = row * s.slab_y
        send_ref[:, start : start + s.slab_y, :] = lines.reshape(s.parts, s.slab_y, s.z)


def fold(dots):
    half = dots.shape[0] // 2
    middle = dots.shape[1] // 2
    folded = dots + pltpu.roll(dots, middle, 1)
    return jnp.where(lane_numbers((half, dots.shape[1])) < middle, folded[:half], folded[half:])


def band_dots(all_bands, flat):
    sums = [
        jnp.sum(all_bands[band] * flat, axis=0, keepdims=True)
        for band in range(all_bands.shape[0])
    ]
    return jnp.concatenate(sums, axis=0)


def band_sum(all_bands, weights):
    total = weights[0:1, :] * all_bands[0]
    for band in range(1, all_bands.shape[0]):
        total = total + weights[band : band + 1, :] * all_bands[band]
    return total


def total_weights(parts, coef_total):
    summed = jnp.sum(parts, axis=0) * (1.0 / coef_total)
    early = lane_numbers(summed.shape) < summed.shape[1] // 2
    halves = [
        jnp.sum(jnp.where(early, summed, 0.0), axis=1, keepdims=True),
        jnp.sum(jnp.where(early, 0.0, summed), axis=1, keepdims=True),
    ]
    weights = jnp.concatenate(halves, axis=0)
    return jnp.broadcast_to(weights, (weights.shape[0], summed.shape[1]))


def wave_energy(wave_number, points):
    folded = jnp.minimum(wave_number, points - wave_number).astype(F32)
    return 4.0 * (folded * (1.0 / points)) ** 2


def start_kernel(s, part_ref, slot_ref, energy_any, psi_any, index_any, tx_any,
                 send_ref, inverse_ref, depth_ref, diag_ref,
                 energy_ref, psi_ref, index_ref, tx_ref, sems):
    copies = [
        pltpu.make_async_copy(source, target, sems.at[number])
        for number, (source, target) in enumerate(
            ((index_any, index_ref), (energy_any, energy_ref), (psi_any, psi_ref), (tx_any, tx_ref))
        )
    ]
    for copy in copies:
        copy.start()
    for copy in copies:
        copy.wait()
    depth = index_ref[...] % s.z
    depth_ref[...] = depth
    turned = depth.T
    cells = lax.broadcasted_iota(jnp.int32, (s.z, s.x), 0)
    for ky in range(s.slab_y):
        inverse = jnp.full((s.z, s.x), -1, jnp.int32)
        for c in range(s.c):
            lane = ky * s.c + c
            inverse = jnp.where(turned[lane : lane + 1, :] == cells, lane, inverse)
        inverse_ref[ky] = inverse.T
    wave_x = lax.broadcasted_iota(jnp.int32, depth.shape, 0)
    wave_y = part_ref[0] * s.slab_y + lane_numbers(depth.shape) // s.c
    kinetic = wave_energy(wave_x, s.x) + wave_energy(wave_y, s.y) + wave_energy(depth, s.z)
    diag_ref[...] = 1.0 / (kinetic - energy_ref[slot_ref[0]])
    send_lines(s, psi_ref[...], inverse_ref, tx_ref[...], send_ref)


def band_kernel(s, recv_ref, local_ref, tyl_ref, tzr_ref, image_ref, grid_ref):
    table_y, table_z = tyl_ref[...], tzr_ref[...]
    group = min(s.slab_x, GROUP)
    for first in range(0, s.slab_x, group):
        inner = slabs_in(s, recv_ref, range(first, first + group), table_y)
        rows = pl.ds(first * s.y, group * s.y)
        grid = from_right(inner, table_z)
        grid_ref[rows, :] = grid
        outer = from_right(local_ref[rows, :] * grid, table_z)
        slabs_out(s, outer, table_y, image_ref, range(first, first + group))


def driving_kernel(s, pert_ref, grid_ref, trial_ref, tyl_ref, tzr_ref, send_ref):
    table_y, table_z = tyl_ref[...], tzr_ref[...]
    group = min(s.slab_x, GROUP)
    for first in range(0, s.slab_x, group):
        rows = pl.ds(first * s.y, group * s.y)
        outer = from_right(trial_ref[pert_ref[0], rows, :] * grid_ref[rows, :], table_z)
        slabs_out(s, outer, table_y, send_ref, range(first, first + group))


def image_kernel(s, recv_ref, depth_ref, tx_ref, image_ref):
    image_ref[...] = read_lines(s, recv_ref, depth_ref[...], tx_ref[...])


def project_kernel(s, recv_ref, depth_ref, all_ref, tx_ref, driving_ref, dots_ref):
    driving = read_lines(s, recv_ref, depth_ref[...], tx_ref[...])
    driving_ref[...] = driving
    dots = fold(band_dots(all_ref, driving))
    dots_ref[...] = jnp.broadcast_to(dots[None], dots_ref.shape)


def first_kernel(s, coef_total, dots_ref, driving_ref, all_ref, diag_ref, inverse_ref,
                 tx_ref, send_ref, start_ref):
    weights = total_weights(dots_ref[...], coef_total)
    start = band_sum(all_ref, weights) - driving_ref[...]
    start_ref[...] = start
    send_lines(s, start * diag_ref[...], inverse_ref, tx_ref[...], send_ref)


def potential_kernel(s, dots_ref, *refs):
    dots = dots_ref[...]
    block = s.slab_x * s.slab_y
    apply_potential(s, *refs)
    refs[-1][:, block:, :] = jnp.broadcast_to(dots[None], (s.parts,) + dots.shape)


def apply_potential(s, recv_ref, local_ref, tyl_ref, tzr_ref, send_ref):
    table_y, table_z = tyl_ref[...], tzr_ref[...]
    group = min(s.slab_x, GROUP)
    for first in range(0, s.slab_x, group):
        inner = slabs_in(s, recv_ref, range(first, first + group), table_y)
        rows = pl.ds(first * s.y, group * s.y)
        grid = from_right(inner, table_z)
        outer = from_right(local_ref[rows, :] * grid, table_z)
        slabs_out(s, outer, table_y, send_ref, range(first, first + group))


def state_dots(bands, images, diag, state):
    return fold(band_dots(bands, state) + band_dots(images, diag * state))


def first_potential_kernel(s, other_ref, *refs):
    apply_potential(s, *refs)


def first_dots_kernel(s, held_ref, all_ref, image_ref, diag_ref, start_ref, send_ref):
    dots = state_dots(all_ref, image_ref, diag_ref[...], start_ref[...])
    block = s.slab_x * s.slab_y
    send_ref[:, block:, :] = jnp.broadcast_to(dots[None], (s.parts,) + dots.shape)


def update_kernel(s, coef_total, last, pert_ref, recv_ref, start_ref, depth_ref, all_ref,
                  image_ref, diag_ref, inverse_ref, tx_ref, own_ref, other_ref, send_ref, dots_ref=None):
    block = s.slab_x * s.slab_y
    table_x = tx_ref[...]
    weights = total_weights(recv_ref[:, block:, :], coef_total)
    change = read_lines(s, recv_ref, depth_ref[...], table_x)
    diag = diag_ref[...]
    state = start_ref[...] - change + band_sum(all_ref, weights)
    response = state * diag
    send_lines(s, response, inverse_ref, table_x, send_ref)
    if not last:
        dots_ref[...] = state_dots(all_ref, image_ref, diag, state)
        return
    own = jnp.sum(own_ref[...] * response, axis=0, keepdims=True)
    other = jnp.sum(other_ref[...] * response, axis=0, keepdims=True)
    lead = pert_ref[0] == 0
    rest = jnp.zeros((6, own.shape[1]), F32)
    sums = jnp.concatenate(
        [jnp.where(lead, own, other), jnp.where(lead, other, own), rest], axis=0
    )
    send_ref[:, block:, :] = jnp.broadcast_to(sums[None], (s.parts,) + sums.shape)


def density_kernel(s, bands, core_ref, recv_ref, grid_ref, tyl_ref, tzr_ref, send_ref):
    table_y, table_z = tyl_ref[...], tzr_ref[...]
    group = min(s.slab_x, GROUP)
    keep = s.y // bands
    for first in range(0, s.slab_x, group):
        inner = slabs_in(s, recv_ref, range(first, first + group), table_y)
        rows = pl.ds(first * s.y, group * s.y)
        density = 2.0 * grid_ref[rows, :] * from_right(inner, table_z)
        for row in range(group):
            for band in range(bands):
                start = row * s.y + band * keep
                place = (first + row) * keep
                slot = core_ref[0] if band % 2 == 0 else 1 - core_ref[0]
                send_ref[slot, band // 2, place : place + keep, :] = density[start : start + keep]
    sums = jnp.sum(recv_ref[:, s.slab_x * s.slab_y :, :], axis=0)
    send_ref[:, :, s.slab_x * keep :, :] = jnp.broadcast_to(
        sums[None, None], (2, bands // 2) + sums.shape
    )


def final_kernel(s, rows, recv_ref, density_ref, sums_ref):
    total = jnp.sum(recv_ref[...], axis=0)
    density_ref[...] = total[:rows]
    lanes = jnp.sum(total[rows:], axis=1, keepdims=True)
    sums_ref[...] = jnp.broadcast_to(lanes, sums_ref.shape)


def call(kernel, out_shape, scalars=0, name=None, aliases=None):
    smem = pl.BlockSpec(memory_space=pltpu.SMEM)
    vmem = pl.BlockSpec(memory_space=pltpu.VMEM)

    def run(*operands):
        return pl.pallas_call(
            kernel,
            out_shape=out_shape,
            in_specs=[smem] * scalars + [vmem] * (len(operands) - scalars),
            out_specs=jax.tree.map(lambda _: vmem, out_shape),
            compiler_params=pltpu.CompilerParams(vmem_limit_bytes=VMEM_LIMIT),
            input_output_aliases=aliases or {},
            name=name,
        )(*operands)

    return run


def shape(*sizes, dtype=F32):
    return jax.ShapeDtypeStruct(sizes, dtype)


def per_device(trial_potential, local_potential, psi_coef, band_energy, band_slot, pw_index):
    parts = lax.axis_size("pw")
    band_count = lax.axis_size("band")
    slab_x, size_y, size_z = local_potential.shape
    size_x = slab_x * parts
    coef_count = psi_coef.shape[0]
    coef_total = coef_count * parts
    total_bands = band_energy.shape[0]
    total_perts = trial_potential.shape[0]
    slab_y = size_y // parts
    s = Sizes(size_x, size_y, size_z, parts, coef_count // (size_x * slab_y))
    block = slab_x * slab_y
    flat = (size_x, slab_y * s.c)
    pert = lax.axis_index("pert").astype(jnp.int32)
    part = lax.axis_index("pw").astype(jnp.int32)
    core = lax.axis_index("band").astype(jnp.int32) & 1
    own_column = lax.broadcasted_iota(jnp.int32, (total_perts, total_perts), 1) == pert
    part, pert, core, own_column, slot = lax.optimization_barrier(
        (part.reshape(1), pert.reshape(1), core.reshape(1), own_column, band_slot)
    )

    table_x = jnp.asarray(left_table(size_x))
    table_y = jnp.asarray(left_table(size_y))
    table_z = jnp.asarray(right_table(size_z))

    def exchange(values):
        return lax.all_to_all(values, "pw", split_axis=0, concat_axis=0, tiled=True)

    psi = psi_coef.reshape(flat)
    index = pw_index.reshape(flat)
    all_psi = lax.all_gather(psi, "band", axis=0)
    anywhere = pl.BlockSpec(memory_space=pltpu.HBM)
    smem = pl.BlockSpec(memory_space=pltpu.SMEM)
    vmem = pl.BlockSpec(memory_space=pltpu.VMEM)
    send, inverse, depth, diag = pl.pallas_call(
        partial(start_kernel, s),
        out_shape=(
            shape(parts, block, size_z),
            shape(slab_y, size_x, size_z, dtype=jnp.int32),
            shape(*flat, dtype=jnp.int32),
            shape(*flat),
        ),
        in_specs=[smem, smem] + [anywhere] * 4,
        out_specs=(vmem,) * 4,
        scratch_shapes=[
            pltpu.SMEM(band_energy.shape, F32),
            pltpu.VMEM(flat, F32),
            pltpu.VMEM(flat, jnp.int32),
            pltpu.VMEM(table_x.shape, BF16),
            pltpu.SemaphoreType.DMA((4,)),
        ],
        compiler_params=pltpu.CompilerParams(vmem_limit_bytes=VMEM_LIMIT),
        name="start",
    )(part, slot, band_energy, psi, index, table_x)
    recv = exchange(send)

    local = local_potential.reshape(slab_x * size_y, size_z)
    trials = trial_potential.reshape(total_perts, slab_x * size_y, size_z)
    send, psi_grid = call(
        partial(band_kernel, s),
        (shape(parts, block, size_z), shape(slab_x * size_y, size_z)),
        0,
        "band",
    )(recv, local, table_y, table_z)
    recv = exchange(send)
    image = call(partial(image_kernel, s), shape(*flat), 0, "image")(recv, depth, table_x)
    all_image = lax.all_gather(image, "band", axis=0)
    psi_grid, image = lax.optimization_barrier((psi_grid, image))
    send = call(partial(driving_kernel, s), shape(parts, block, size_z), 1, "driving")(
        pert, psi_grid, trials, table_y, table_z
    )
    recv = exchange(send)
    driving, dots = call(
        partial(project_kernel, s),
        (shape(*flat), shape(parts, total_bands // 2, size_z)),
        0,
        "project",
    )(recv, depth, all_psi, table_x)
    dots = exchange(dots)
    send, start = call(
        partial(first_kernel, s, coef_total),
        (shape(parts, block, size_z), shape(*flat)),
        0,
        "first",
    )(dots, driving, all_psi, diag, inverse, table_x)
    other = lax.ppermute(driving, "pert", [(0, 1), (1, 0)])
    for iteration in range(ITERS):
        last = iteration == ITERS - 1
        recv = exchange(send)
        out = shape(parts, block + total_bands // 2, size_z)
        if iteration == 0:
            send = call(partial(first_potential_kernel, s), out, 0, "potential")(
                other, recv, local, table_y, table_z
            )
            send, all_image = lax.optimization_barrier((send, all_image))
            send = call(partial(first_dots_kernel, s), out, 0, "dots", {0: 0})(
                send, all_psi, all_image, diag, start
            )
        else:
            send = call(partial(potential_kernel, s), out, 0, "potential")(
                dots, recv, local, table_y, table_z
            )
        recv = exchange(send)
        if last:
            outs = (shape(parts, block + 8, size_z),)
        else:
            outs = (shape(parts, block, size_z), shape(total_bands // 2, size_z))
        send, *rest = call(partial(update_kernel, s, coef_total, last), outs, 1, "update")(
            pert, recv, start, depth, all_psi, all_image, diag, inverse, table_x, driving,
            other,
        )
        dots = rest[0] if rest else None

    recv = exchange(send)
    rows = slab_x * (size_y // band_count)
    send = call(
        partial(density_kernel, s, band_count),
        shape(2, band_count // 2, rows + 8, size_z),
        1,
        "density",
    )(core, recv, psi_grid, table_y, table_z)
    got = lax.ppermute(send[1], "band", [(band, band ^ 1) for band in range(band_count)])
    near = [[2 * z + c for z in range(band_count // 2)] for c in range(2)]
    recv = lax.all_to_all(
        send[0] + got, "band", split_axis=0, concat_axis=0, tiled=True, axis_index_groups=near
    )
    density, sums = call(
        partial(final_kernel, s, rows), (shape(rows, size_z), shape(8, size_z)), 0, "final"
    )(recv)
    own = sums[:total_perts, :total_perts] * (2.0 / (total_bands * coef_total))
    across = lax.ppermute(own, "pert", [(0, 1), (1, 0)])
    intersections = jnp.where(own_column, own, across)
    return (
        density.reshape(1, slab_x, size_y // band_count, size_z),
        intersections,
    )


def solution(mesh):
    return jax.shard_map(
        per_device,
        mesh=mesh,
        in_specs=(
            P(None, "pw", None, None),
            P("pw", None, None),
            P("pw", "band"),
            P(),
            P("band"),
            P("pw"),
        ),
        out_specs=(P("pert", "pw", "band", None), P()),
        check_vma=False,
    )
```

```python
import math
from functools import partial

import jax
import jax.numpy as jnp
import numpy as np
from jax import lax
from jax.experimental import pallas as pl
from jax.experimental.pallas import tpu as pltpu
from jax.sharding import PartitionSpec as P

ITERS = 3
F32 = jnp.float32
BF16 = jnp.bfloat16
GROUP = 16
VMEM_LIMIT = 16 * 1024 * 1024


def hartley_pieces(points):
    wave_index = np.arange(points)
    angles = (wave_index[:, None] * wave_index[None, :] % points) * (2.0 * math.pi / points)
    table = (np.cos(angles) + np.sin(angles)) / math.sqrt(points)
    high = table.astype(np.float32).astype(jnp.bfloat16)
    low = (table - high.astype(np.float64)).astype(np.float32).astype(jnp.bfloat16)
    return high, low


def left_table(points):
    high, low = hartley_pieces(points)
    return np.concatenate([high, high, low], axis=1)


def right_table(points):
    high, low = hartley_pieces(points)
    return np.concatenate([high, high, low], axis=0)


def stack_pieces(values, axis):
    high = values.astype(BF16)
    low = (values - high.astype(F32)).astype(BF16)
    return jnp.concatenate([high, low, high], axis=axis)


def from_left(table, values):
    return jnp.dot(table, stack_pieces(values, 0), preferred_element_type=F32)


def all_from_left(table, blocks):
    results = []
    for first in range(0, len(blocks), 2):
        pair = blocks[first : first + 2]
        width = pair[0].shape[1]
        wide = from_left(table, jnp.concatenate(pair, axis=1))
        results += [wide[:, n * width : (n + 1) * width] for n in range(len(pair))]
    return results


def from_right(values, table):
    return jnp.dot(stack_pieces(values, 1), table, preferred_element_type=F32)


def pick(values, lanes):
    return jnp.take_along_axis(values, lanes, axis=1, mode="promise_in_bounds")


def lane_numbers(shape):
    return lax.broadcasted_iota(jnp.int32, shape, len(shape) - 1)


class Sizes:
    def __init__(self, size_x, size_y, size_z, parts, per_line):
        self.x, self.y, self.z, self.parts, self.c = size_x, size_y, size_z, parts, per_line
        self.slab_x, self.slab_y = size_x // parts, size_y // parts


def send_lines(s, flat, inverse_ref, table_x, send_ref):
    placed = []
    for ky in range(s.slab_y):
        lanes = inverse_ref[ky]
        placed.append(jnp.where(lanes >= 0, pick(flat, jnp.maximum(lanes, 0)), 0.0))
    for ky, lines in enumerate(all_from_left(table_x, placed)):
        for part in range(s.parts):
            rows = lines[part * s.slab_x : (part + 1) * s.slab_x]
            send_ref[part, pl.ds(ky, s.slab_x, s.slab_y), :] = rows


def read_lines(s, recv_ref, depth, table_x):
    result = jnp.zeros((s.x, s.slab_y * s.c), F32)
    group = lane_numbers(result.shape) // s.c
    blocks = [
        jnp.concatenate(
            [
                recv_ref[source, pl.ds(ky, s.slab_x, s.slab_y), :]
                for source in range(s.parts)
            ],
            axis=0,
        )
        for ky in range(s.slab_y)
    ]
    for ky, lines in enumerate(all_from_left(table_x, blocks)):
        result = jnp.where(group == ky, pick(lines, depth), result)
    return result


def slabs_in(s, recv_ref, rows, table_y):
    blocks = [
        recv_ref[:, row * s.slab_y : (row + 1) * s.slab_y, :].reshape(s.y, s.z) for row in rows
    ]
    return jnp.concatenate(all_from_left(table_y, blocks), axis=0)


def slabs_out(s, values, table_y, send_ref, rows):
    blocks = [values[n * s.y : (n + 1) * s.y] for n in range(len(rows))]
    for row, lines in zip(rows, all_from_left(table_y, blocks)):
        start = row * s.slab_y
        send_ref[:, start : start + s.slab_y, :] = lines.reshape(s.parts, s.slab_y, s.z)


def fold(dots):
    half = dots.shape[0] // 2
    middle = dots.shape[1] // 2
    folded = dots + pltpu.roll(dots, middle, 1)
    return jnp.where(lane_numbers((half, dots.shape[1])) < middle, folded[:half], folded[half:])


def band_dots(all_bands, flat):
    sums = [
        jnp.sum(all_bands[band] * flat, axis=0, keepdims=True)
        for band in range(all_bands.shape[0])
    ]
    return jnp.concatenate(sums, axis=0)


def band_sum(all_bands, weights):
    total = weights[0:1, :] * all_bands[0]
    for band in range(1, all_bands.shape[0]):
        total = total + weights[band : band + 1, :] * all_bands[band]
    return total


def total_weights(parts, coef_total):
    summed = jnp.sum(parts, axis=0) * (1.0 / coef_total)
    early = lane_numbers(summed.shape) < summed.shape[1] // 2
    halves = [
        jnp.sum(jnp.where(early, summed, 0.0), axis=1, keepdims=True),
        jnp.sum(jnp.where(early, 0.0, summed), axis=1, keepdims=True),
    ]
    weights = jnp.concatenate(halves, axis=0)
    return jnp.broadcast_to(weights, (weights.shape[0], summed.shape[1]))


def wave_energy(wave_number, points):
    folded = jnp.minimum(wave_number, points - wave_number).astype(F32)
    return 4.0 * (folded * (1.0 / points)) ** 2


def start_kernel(s, part_ref, slot_ref, energy_any, psi_any, index_any, tx_any,
                 send_ref, inverse_ref, depth_ref, diag_ref,
                 energy_ref, psi_ref, index_ref, tx_ref, sems):
    copies = [
        pltpu.make_async_copy(source, target, sems.at[number])
        for number, (source, target) in enumerate(
            ((index_any, index_ref), (energy_any, energy_ref), (psi_any, psi_ref), (tx_any, tx_ref))
        )
    ]
    for copy in copies:
        copy.start()
    for copy in copies:
        copy.wait()
    depth = index_ref[...] % s.z
    depth_ref[...] = depth
    turned = depth.T
    cells = lax.broadcasted_iota(jnp.int32, (s.z, s.x), 0)
    for ky in range(s.slab_y):
        inverse = jnp.full((s.z, s.x), -1, jnp.int32)
        for c in range(s.c):
            lane = ky * s.c + c
            inverse = jnp.where(turned[lane : lane + 1, :] == cells, lane, inverse)
        inverse_ref[ky] = inverse.T
    wave_x = lax.broadcasted_iota(jnp.int32, depth.shape, 0)
    wave_y = part_ref[0] * s.slab_y + lane_numbers(depth.shape) // s.c
    kinetic = wave_energy(wave_x, s.x) + wave_energy(wave_y, s.y) + wave_energy(depth, s.z)
    diag_ref[...] = 1.0 / (kinetic - energy_ref[slot_ref[0]])
    send_lines(s, psi_ref[...], inverse_ref, tx_ref[...], send_ref)


def band_kernel(s, recv_ref, local_ref, tyl_ref, tzr_ref, image_ref, grid_ref):
    table_y, table_z = tyl_ref[...], tzr_ref[...]
    group = min(s.slab_x, GROUP)
    for first in range(0, s.slab_x, group):
        inner = slabs_in(s, recv_ref, range(first, first + group), table_y)
        rows = pl.ds(first * s.y, group * s.y)
        grid = from_right(inner, table_z)
        grid_ref[rows, :] = grid
        outer = from_right(local_ref[rows, :] * grid, table_z)
        slabs_out(s, outer, table_y, image_ref, range(first, first + group))


def driving_kernel(s, pert_ref, grid_ref, trial_ref, tyl_ref, tzr_ref, send_ref):
    table_y, table_z = tyl_ref[...], tzr_ref[...]
    group = min(s.slab_x, GROUP)
    for first in range(0, s.slab_x, group):
        rows = pl.ds(first * s.y, group * s.y)
        outer = from_right(trial_ref[pert_ref[0], rows, :] * grid_ref[rows, :], table_z)
        slabs_out(s, outer, table_y, send_ref, range(first, first + group))


def image_kernel(s, recv_ref, depth_ref, tx_ref, image_ref):
    image_ref[...] = read_lines(s, recv_ref, depth_ref[...], tx_ref[...])


def project_kernel(s, recv_ref, depth_ref, all_ref, tx_ref, driving_ref, dots_ref):
    driving = read_lines(s, recv_ref, depth_ref[...], tx_ref[...])
    driving_ref[...] = driving
    dots = fold(band_dots(all_ref, driving))
    dots_ref[...] = jnp.broadcast_to(dots[None], dots_ref.shape)


def first_kernel(s, coef_total, dots_ref, driving_ref, all_ref, diag_ref, inverse_ref,
                 tx_ref, send_ref, start_ref):
    weights = total_weights(dots_ref[...], coef_total)
    start = band_sum(all_ref, weights) - driving_ref[...]
    start_ref[...] = start
    send_lines(s, start * diag_ref[...], inverse_ref, tx_ref[...], send_ref)


def potential_kernel(s, dots_ref, *refs):
    dots = dots_ref[...]
    block = s.slab_x * s.slab_y
    apply_potential(s, *refs)
    refs[-1][:, block:, :] = jnp.broadcast_to(dots[None], (s.parts,) + dots.shape)


def apply_potential(s, recv_ref, local_ref, tyl_ref, tzr_ref, send_ref):
    table_y, table_z = tyl_ref[...], tzr_ref[...]
    group = min(s.slab_x, GROUP)
    for first in range(0, s.slab_x, group):
        inner = slabs_in(s, recv_ref, range(first, first + group), table_y)
        rows = pl.ds(first * s.y, group * s.y)
        grid = from_right(inner, table_z)
        outer = from_right(local_ref[rows, :] * grid, table_z)
        slabs_out(s, outer, table_y, send_ref, range(first, first + group))


def state_dots(bands, images, diag, state):
    return fold(band_dots(bands, state) + band_dots(images, diag * state))


def first_potential_kernel(s, other_ref, *refs):
    apply_potential(s, *refs)


def first_dots_kernel(s, held_ref, all_ref, image_ref, diag_ref, start_ref, send_ref):
    dots = state_dots(all_ref, image_ref, diag_ref[...], start_ref[...])
    block = s.slab_x * s.slab_y
    send_ref[:, block:, :] = jnp.broadcast_to(dots[None], (s.parts,) + dots.shape)


def update_kernel(s, coef_total, last, pert_ref, recv_ref, start_ref, depth_ref, all_ref,
                  image_ref, diag_ref, inverse_ref, tx_ref, own_ref, even_ref, odd_ref, send_ref, dots_ref=None):
    block = s.slab_x * s.slab_y
    table_x = tx_ref[...]
    weights = total_weights(recv_ref[:, block:, :], coef_total)
    change = read_lines(s, recv_ref, depth_ref[...], table_x)
    diag = diag_ref[...]
    state = start_ref[...] - change + band_sum(all_ref, weights)
    response = state * diag
    send_lines(s, response, inverse_ref, table_x, send_ref)
    if not last:
        dots_ref[...] = state_dots(all_ref, image_ref, diag, state)
        return
    own = jnp.sum(own_ref[...] * response, axis=0, keepdims=True)
    other = jnp.sum((even_ref[...] + odd_ref[...]) * response, axis=0, keepdims=True)
    lead = pert_ref[0] == 0
    rest = jnp.zeros((6, own.shape[1]), F32)
    sums = jnp.concatenate(
        [jnp.where(lead, own, other), jnp.where(lead, other, own), rest], axis=0
    )
    send_ref[:, block:, :] = jnp.broadcast_to(sums[None], (s.parts,) + sums.shape)


def density_kernel(s, bands, core_ref, recv_ref, grid_ref, tyl_ref, tzr_ref, send_ref):
    table_y, table_z = tyl_ref[...], tzr_ref[...]
    group = min(s.slab_x, GROUP)
    keep = s.y // bands
    for first in range(0, s.slab_x, group):
        inner = slabs_in(s, recv_ref, range(first, first + group), table_y)
        rows = pl.ds(first * s.y, group * s.y)
        density = 2.0 * grid_ref[rows, :] * from_right(inner, table_z)
        for row in range(group):
            for band in range(bands):
                start = row * s.y + band * keep
                place = (first + row) * keep
                slot = core_ref[0] if band % 2 == 0 else 1 - core_ref[0]
                send_ref[slot, band // 2, place : place + keep, :] = density[start : start + keep]
    sums = jnp.sum(recv_ref[:, s.slab_x * s.slab_y :, :], axis=0)
    send_ref[:, :, s.slab_x * keep :, :] = jnp.broadcast_to(
        sums[None, None], (2, bands // 2) + sums.shape
    )


def final_kernel(s, rows, recv_ref, density_ref, sums_ref):
    total = jnp.sum(recv_ref[...], axis=0)
    density_ref[...] = total[:rows]
    lanes = jnp.sum(total[rows:], axis=1, keepdims=True)
    sums_ref[...] = jnp.broadcast_to(lanes, sums_ref.shape)


def call(kernel, out_shape, scalars=0, name=None, aliases=None):
    smem = pl.BlockSpec(memory_space=pltpu.SMEM)
    vmem = pl.BlockSpec(memory_space=pltpu.VMEM)

    def run(*operands):
        return pl.pallas_call(
            kernel,
            out_shape=out_shape,
            in_specs=[smem] * scalars + [vmem] * (len(operands) - scalars),
            out_specs=jax.tree.map(lambda _: vmem, out_shape),
            compiler_params=pltpu.CompilerParams(vmem_limit_bytes=VMEM_LIMIT),
            input_output_aliases=aliases or {},
            name=name,
        )(*operands)

    return run


def shape(*sizes, dtype=F32):
    return jax.ShapeDtypeStruct(sizes, dtype)


def per_device(trial_potential, local_potential, psi_coef, band_energy, band_slot, pw_index):
    parts = lax.axis_size("pw")
    band_count = lax.axis_size("band")
    slab_x, size_y, size_z = local_potential.shape
    size_x = slab_x * parts
    coef_count = psi_coef.shape[0]
    coef_total = coef_count * parts
    total_bands = band_energy.shape[0]
    total_perts = trial_potential.shape[0]
    slab_y = size_y // parts
    s = Sizes(size_x, size_y, size_z, parts, coef_count // (size_x * slab_y))
    block = slab_x * slab_y
    flat = (size_x, slab_y * s.c)
    pert = lax.axis_index("pert").astype(jnp.int32)
    part = lax.axis_index("pw").astype(jnp.int32)
    core = lax.axis_index("band").astype(jnp.int32) & 1
    own_column = lax.broadcasted_iota(jnp.int32, (total_perts, total_perts), 1) == pert
    part, pert, core, own_column, slot = lax.optimization_barrier(
        (part.reshape(1), pert.reshape(1), core.reshape(1), own_column, band_slot)
    )

    table_x = jnp.asarray(left_table(size_x))
    table_y = jnp.asarray(left_table(size_y))
    table_z = jnp.asarray(right_table(size_z))

    def exchange(values):
        return lax.all_to_all(values, "pw", split_axis=0, concat_axis=0, tiled=True)

    psi = psi_coef.reshape(flat)
    index = pw_index.reshape(flat)
    all_psi = lax.all_gather(psi, "band", axis=0)
    anywhere = pl.BlockSpec(memory_space=pltpu.HBM)
    smem = pl.BlockSpec(memory_space=pltpu.SMEM)
    vmem = pl.BlockSpec(memory_space=pltpu.VMEM)
    send, inverse, depth, diag = pl.pallas_call(
        partial(start_kernel, s),
        out_shape=(
            shape(parts, block, size_z),
            shape(slab_y, size_x, size_z, dtype=jnp.int32),
            shape(*flat, dtype=jnp.int32),
            shape(*flat),
        ),
        in_specs=[smem, smem] + [anywhere] * 4,
        out_specs=(vmem,) * 4,
        scratch_shapes=[
            pltpu.SMEM(band_energy.shape, F32),
            pltpu.VMEM(flat, F32),
            pltpu.VMEM(flat, jnp.int32),
            pltpu.VMEM(table_x.shape, BF16),
            pltpu.SemaphoreType.DMA((4,)),
        ],
        compiler_params=pltpu.CompilerParams(vmem_limit_bytes=VMEM_LIMIT),
        name="start",
    )(part, slot, band_energy, psi, index, table_x)
    recv = exchange(send)

    local = local_potential.reshape(slab_x * size_y, size_z)
    trials = trial_potential.reshape(total_perts, slab_x * size_y, size_z)
    send, psi_grid = call(
        partial(band_kernel, s),
        (shape(parts, block, size_z), shape(slab_x * size_y, size_z)),
        0,
        "band",
    )(recv, local, table_y, table_z)
    recv = exchange(send)
    image = call(partial(image_kernel, s), shape(*flat), 0, "image")(recv, depth, table_x)
    all_image = lax.all_gather(image, "band", axis=0)
    psi_grid, image = lax.optimization_barrier((psi_grid, image))
    send = call(partial(driving_kernel, s), shape(parts, block, size_z), 1, "driving")(
        pert, psi_grid, trials, table_y, table_z
    )
    recv = exchange(send)
    driving, dots = call(
        partial(project_kernel, s),
        (shape(*flat), shape(parts, total_bands // 2, size_z)),
        0,
        "project",
    )(recv, depth, all_psi, table_x)
    dots = exchange(dots)
    send, start = call(
        partial(first_kernel, s, coef_total),
        (shape(parts, block, size_z), shape(*flat)),
        0,
        "first",
    )(dots, driving, all_psi, diag, inverse, table_x)
    even, odd = (
        [(i * band_count + b, (1 - i) * band_count + b) for i in range(2) for b in group]
        for group in (range(0, band_count, 2), range(1, band_count, 2))
    )
    other_odd = lax.ppermute(driving, ("pert", "band"), odd)
    for iteration in range(ITERS):
        last = iteration == ITERS - 1
        recv = exchange(send)
        out = shape(parts, block + total_bands // 2, size_z)
        if iteration == 0:
            send = call(partial(first_potential_kernel, s), out, 0, "potential")(
                other_odd, recv, local, table_y, table_z
            )
            send, all_image, driving = lax.optimization_barrier((send, all_image, driving))
            other_even = lax.ppermute(driving, ("pert", "band"), even)
            send = call(partial(first_dots_kernel, s), out, 0, "dots", {0: 0})(
                send, all_psi, all_image, diag, start
            )
            send, other_even = lax.optimization_barrier((send, other_even))
        else:
            send = call(partial(potential_kernel, s), out, 0, "potential")(
                dots, recv, local, table_y, table_z
            )
        recv = exchange(send)
        if last:
            outs = (shape(parts, block + 8, size_z),)
        else:
            outs = (shape(parts, block, size_z), shape(total_bands // 2, size_z))
        send, *rest = call(partial(update_kernel, s, coef_total, last), outs, 1, "update")(
            pert, recv, start, depth, all_psi, all_image, diag, inverse, table_x, driving,
            other_even, other_odd,
        )
        dots = rest[0] if rest else None

    recv = exchange(send)
    rows = slab_x * (size_y // band_count)
    send = call(
        partial(density_kernel, s, band_count),
        shape(2, band_count // 2, rows + 8, size_z),
        1,
        "density",
    )(core, recv, psi_grid, table_y, table_z)
    got = lax.ppermute(send[1], "band", [(band, band ^ 1) for band in range(band_count)])
    near = [[2 * z + c for z in range(band_count // 2)] for c in range(2)]
    recv = lax.all_to_all(
        send[0] + got, "band", split_axis=0, concat_axis=0, tiled=True, axis_index_groups=near
    )
    density, sums = call(
        partial(final_kernel, s, rows), (shape(rows, size_z), shape(8, size_z)), 0, "final"
    )(recv)
    own = sums[:total_perts, :total_perts] * (2.0 / (total_bands * coef_total))
    across = lax.ppermute(own, "pert", [(0, 1), (1, 0)])
    intersections = jnp.where(own_column, own, across)
    return (
        density.reshape(1, slab_x, size_y // band_count, size_z),
        intersections,
    )


def solution(mesh):
    return jax.shard_map(
        per_device,
        mesh=mesh,
        in_specs=(
            P(None, "pw", None, None),
            P("pw", None, None),
            P("pw", "band"),
            P(),
            P("band"),
            P("pw"),
        ),
        out_specs=(P("pert", "pw", "band", None), P()),
        check_vma=False,
    )
```

```python
import math
from functools import partial

import jax
import jax.numpy as jnp
import numpy as np
from jax import lax
from jax.experimental import pallas as pl
from jax.experimental.pallas import tpu as pltpu
from jax.sharding import PartitionSpec as P

ITERS = 3
F32 = jnp.float32
BF16 = jnp.bfloat16
GROUP = 16
VMEM_LIMIT = 16 * 1024 * 1024


def hartley_pieces(points):
    wave_index = np.arange(points)
    angles = (wave_index[:, None] * wave_index[None, :] % points) * (2.0 * math.pi / points)
    table = (np.cos(angles) + np.sin(angles)) / math.sqrt(points)
    high = table.astype(np.float32).astype(jnp.bfloat16)
    low = (table - high.astype(np.float64)).astype(np.float32).astype(jnp.bfloat16)
    return high, low


def left_table(points):
    high, low = hartley_pieces(points)
    return np.concatenate([high, high, low], axis=1)


def right_table(points):
    high, low = hartley_pieces(points)
    return np.concatenate([high, high, low], axis=0)


def stack_pieces(values, axis):
    high = values.astype(BF16)
    low = (values - high.astype(F32)).astype(BF16)
    return jnp.concatenate([high, low, high], axis=axis)


def from_left(table, values):
    return jnp.dot(table, stack_pieces(values, 0), preferred_element_type=F32)


def all_from_left(table, blocks):
    results = []
    for first in range(0, len(blocks), 2):
        pair = blocks[first : first + 2]
        width = pair[0].shape[1]
        wide = from_left(table, jnp.concatenate(pair, axis=1))
        results += [wide[:, n * width : (n + 1) * width] for n in range(len(pair))]
    return results


def from_right(values, table):
    return jnp.dot(stack_pieces(values, 1), table, preferred_element_type=F32)


def pick(values, lanes):
    return jnp.take_along_axis(values, lanes, axis=1, mode="promise_in_bounds")


def lane_numbers(shape):
    return lax.broadcasted_iota(jnp.int32, shape, len(shape) - 1)


class Sizes:
    def __init__(self, size_x, size_y, size_z, parts, per_line):
        self.x, self.y, self.z, self.parts, self.c = size_x, size_y, size_z, parts, per_line
        self.slab_x, self.slab_y = size_x // parts, size_y // parts


def send_lines(s, flat, inverse_ref, table_x, send_ref):
    placed = []
    for ky in range(s.slab_y):
        lanes = inverse_ref[ky]
        placed.append(jnp.where(lanes >= 0, pick(flat, jnp.maximum(lanes, 0)), 0.0))
    for ky, lines in enumerate(all_from_left(table_x, placed)):
        for part in range(s.parts):
            rows = lines[part * s.slab_x : (part + 1) * s.slab_x]
            send_ref[part, pl.ds(ky, s.slab_x, s.slab_y), :] = rows


def read_lines(s, recv_ref, depth, table_x):
    result = jnp.zeros((s.x, s.slab_y * s.c), F32)
    group = lane_numbers(result.shape) // s.c
    blocks = [
        jnp.concatenate(
            [
                recv_ref[source, pl.ds(ky, s.slab_x, s.slab_y), :]
                for source in range(s.parts)
            ],
            axis=0,
        )
        for ky in range(s.slab_y)
    ]
    for ky, lines in enumerate(all_from_left(table_x, blocks)):
        result = jnp.where(group == ky, pick(lines, depth), result)
    return result


def slabs_in(s, recv_ref, rows, table_y):
    blocks = [
        recv_ref[:, row * s.slab_y : (row + 1) * s.slab_y, :].reshape(s.y, s.z) for row in rows
    ]
    return jnp.concatenate(all_from_left(table_y, blocks), axis=0)


def slabs_out(s, values, table_y, send_ref, rows):
    blocks = [values[n * s.y : (n + 1) * s.y] for n in range(len(rows))]
    for row, lines in zip(rows, all_from_left(table_y, blocks)):
        start = row * s.slab_y
        send_ref[:, start : start + s.slab_y, :] = lines.reshape(s.parts, s.slab_y, s.z)


def fold(dots):
    half = dots.shape[0] // 2
    middle = dots.shape[1] // 2
    folded = dots + pltpu.roll(dots, middle, 1)
    return jnp.where(lane_numbers((half, dots.shape[1])) < middle, folded[:half], folded[half:])


def band_dots(all_bands, flat):
    sums = [
        jnp.sum(all_bands[band] * flat, axis=0, keepdims=True)
        for band in range(all_bands.shape[0])
    ]
    return jnp.concatenate(sums, axis=0)


def band_sum(all_bands, weights):
    total = weights[0:1, :] * all_bands[0]
    for band in range(1, all_bands.shape[0]):
        total = total + weights[band : band + 1, :] * all_bands[band]
    return total


def total_weights(parts, coef_total):
    summed = jnp.sum(parts, axis=0) * (1.0 / coef_total)
    early = lane_numbers(summed.shape) < summed.shape[1] // 2
    halves = [
        jnp.sum(jnp.where(early, summed, 0.0), axis=1, keepdims=True),
        jnp.sum(jnp.where(early, 0.0, summed), axis=1, keepdims=True),
    ]
    weights = jnp.concatenate(halves, axis=0)
    return jnp.broadcast_to(weights, (weights.shape[0], summed.shape[1]))


def wave_energy(wave_number, points):
    folded = jnp.minimum(wave_number, points - wave_number).astype(F32)
    return 4.0 * (folded * (1.0 / points)) ** 2


def start_kernel(s, part_ref, slot_ref, energy_any, psi_any, index_any, tx_any,
                 send_ref, inverse_ref, depth_ref, diag_ref,
                 energy_ref, psi_ref, index_ref, tx_ref, sems):
    copies = [
        pltpu.make_async_copy(source, target, sems.at[number])
        for number, (source, target) in enumerate(
            ((index_any, index_ref), (energy_any, energy_ref), (psi_any, psi_ref), (tx_any, tx_ref))
        )
    ]
    for copy in copies:
        copy.start()
    for copy in copies:
        copy.wait()
    depth = index_ref[...] % s.z
    depth_ref[...] = depth
    turned = depth.T
    cells = lax.broadcasted_iota(jnp.int32, (s.z, s.x), 0)
    for ky in range(s.slab_y):
        inverse = jnp.full((s.z, s.x), -1, jnp.int32)
        for c in range(s.c):
            lane = ky * s.c + c
            inverse = jnp.where(turned[lane : lane + 1, :] == cells, lane, inverse)
        inverse_ref[ky] = inverse.T
    wave_x = lax.broadcasted_iota(jnp.int32, depth.shape, 0)
    wave_y = part_ref[0] * s.slab_y + lane_numbers(depth.shape) // s.c
    kinetic = wave_energy(wave_x, s.x) + wave_energy(wave_y, s.y) + wave_energy(depth, s.z)
    diag_ref[...] = 1.0 / (kinetic - energy_ref[slot_ref[0]])
    send_lines(s, psi_ref[...], inverse_ref, tx_ref[...], send_ref)


def band_kernel(s, recv_ref, local_ref, tyl_ref, tzr_ref, image_ref, grid_ref):
    table_y, table_z = tyl_ref[...], tzr_ref[...]
    group = min(s.slab_x, GROUP)
    for first in range(0, s.slab_x, group):
        inner = slabs_in(s, recv_ref, range(first, first + group), table_y)
        rows = pl.ds(first * s.y, group * s.y)
        grid = from_right(inner, table_z)
        grid_ref[rows, :] = grid
        outer = from_right(local_ref[rows, :] * grid, table_z)
        slabs_out(s, outer, table_y, image_ref, range(first, first + group))


def driving_kernel(s, pert_ref, grid_ref, trial_ref, tyl_ref, tzr_ref, send_ref):
    table_y, table_z = tyl_ref[...], tzr_ref[...]
    group = min(s.slab_x, GROUP)
    for first in range(0, s.slab_x, group):
        rows = pl.ds(first * s.y, group * s.y)
        outer = from_right(trial_ref[pert_ref[0], rows, :] * grid_ref[rows, :], table_z)
        slabs_out(s, outer, table_y, send_ref, range(first, first + group))


def image_kernel(s, recv_ref, depth_ref, tx_ref, image_ref):
    image_ref[...] = read_lines(s, recv_ref, depth_ref[...], tx_ref[...])


def project_kernel(s, recv_ref, depth_ref, all_ref, tx_ref, driving_ref, dots_ref):
    driving = read_lines(s, recv_ref, depth_ref[...], tx_ref[...])
    driving_ref[...] = driving
    dots = fold(band_dots(all_ref, driving))
    dots_ref[...] = jnp.broadcast_to(dots[None], dots_ref.shape)


def first_kernel(s, coef_total, dots_ref, driving_ref, all_ref, diag_ref, inverse_ref,
                 tx_ref, send_ref, start_ref):
    weights = total_weights(dots_ref[...], coef_total)
    start = band_sum(all_ref, weights) - driving_ref[...]
    start_ref[...] = start
    send_lines(s, start * diag_ref[...], inverse_ref, tx_ref[...], send_ref)


def potential_kernel(s, dots_ref, *refs):
    dots = dots_ref[...]
    block = s.slab_x * s.slab_y
    apply_potential(s, *refs)
    refs[-1][:, block:, :] = jnp.broadcast_to(dots[None], (s.parts,) + dots.shape)


def apply_potential(s, recv_ref, local_ref, tyl_ref, tzr_ref, send_ref):
    table_y, table_z = tyl_ref[...], tzr_ref[...]
    group = min(s.slab_x, GROUP)
    for first in range(0, s.slab_x, group):
        inner = slabs_in(s, recv_ref, range(first, first + group), table_y)
        rows = pl.ds(first * s.y, group * s.y)
        grid = from_right(inner, table_z)
        outer = from_right(local_ref[rows, :] * grid, table_z)
        slabs_out(s, outer, table_y, send_ref, range(first, first + group))


def state_dots(bands, images, diag, state):
    return fold(band_dots(bands, state) + band_dots(images, diag * state))


def first_dots_kernel(s, held_ref, all_ref, image_ref, diag_ref, start_ref, send_ref):
    dots = state_dots(all_ref, image_ref, diag_ref[...], start_ref[...])
    block = s.slab_x * s.slab_y
    send_ref[:, block:, :] = jnp.broadcast_to(dots[None], (s.parts,) + dots.shape)


def update_kernel(s, coef_total, last, pert_ref, recv_ref, start_ref, depth_ref, all_ref,
                  image_ref, diag_ref, inverse_ref, tx_ref, own_ref, even_ref, odd_ref, send_ref, dots_ref=None):
    block = s.slab_x * s.slab_y
    table_x = tx_ref[...]
    weights = total_weights(recv_ref[:, block:, :], coef_total)
    change = read_lines(s, recv_ref, depth_ref[...], table_x)
    diag = diag_ref[...]
    state = start_ref[...] - change + band_sum(all_ref, weights)
    response = state * diag
    send_lines(s, response, inverse_ref, table_x, send_ref)
    if not last:
        dots_ref[...] = state_dots(all_ref, image_ref, diag, state)
        return
    own = jnp.sum(own_ref[...] * response, axis=0, keepdims=True)
    other = jnp.sum((even_ref[...] + odd_ref[...]) * response, axis=0, keepdims=True)
    lead = pert_ref[0] == 0
    rest = jnp.zeros((6, own.shape[1]), F32)
    sums = jnp.concatenate(
        [jnp.where(lead, own, other), jnp.where(lead, other, own), rest], axis=0
    )
    send_ref[:, block:, :] = jnp.broadcast_to(sums[None], (s.parts,) + sums.shape)


def density_kernel(s, bands, core_ref, recv_ref, grid_ref, tyl_ref, tzr_ref, send_ref):
    table_y, table_z = tyl_ref[...], tzr_ref[...]
    group = min(s.slab_x, GROUP)
    keep = s.y // bands
    for first in range(0, s.slab_x, group):
        inner = slabs_in(s, recv_ref, range(first, first + group), table_y)
        rows = pl.ds(first * s.y, group * s.y)
        density = 2.0 * grid_ref[rows, :] * from_right(inner, table_z)
        for row in range(group):
            for band in range(bands):
                start = row * s.y + band * keep
                place = (first + row) * keep
                slot = core_ref[0] if band % 2 == 0 else 1 - core_ref[0]
                send_ref[slot, band // 2, place : place + keep, :] = density[start : start + keep]
    sums = jnp.sum(recv_ref[:, s.slab_x * s.slab_y :, :], axis=0)
    send_ref[:, :, s.slab_x * keep :, :] = jnp.broadcast_to(
        sums[None, None], (2, bands // 2) + sums.shape
    )


def final_kernel(s, rows, recv_ref, density_ref, sums_ref):
    total = jnp.sum(recv_ref[...], axis=0)
    density_ref[...] = total[:rows]
    lanes = jnp.sum(total[rows:], axis=1, keepdims=True)
    sums_ref[...] = jnp.broadcast_to(lanes, sums_ref.shape)


def call(kernel, out_shape, scalars=0, name=None, aliases=None):
    smem = pl.BlockSpec(memory_space=pltpu.SMEM)
    vmem = pl.BlockSpec(memory_space=pltpu.VMEM)

    def run(*operands):
        return pl.pallas_call(
            kernel,
            out_shape=out_shape,
            in_specs=[smem] * scalars + [vmem] * (len(operands) - scalars),
            out_specs=jax.tree.map(lambda _: vmem, out_shape),
            compiler_params=pltpu.CompilerParams(vmem_limit_bytes=VMEM_LIMIT),
            input_output_aliases=aliases or {},
            name=name,
        )(*operands)

    return run


def shape(*sizes, dtype=F32):
    return jax.ShapeDtypeStruct(sizes, dtype)


def per_device(trial_potential, local_potential, psi_coef, band_energy, band_slot, pw_index):
    parts = lax.axis_size("pw")
    band_count = lax.axis_size("band")
    slab_x, size_y, size_z = local_potential.shape
    size_x = slab_x * parts
    coef_count = psi_coef.shape[0]
    coef_total = coef_count * parts
    total_bands = band_energy.shape[0]
    total_perts = trial_potential.shape[0]
    slab_y = size_y // parts
    s = Sizes(size_x, size_y, size_z, parts, coef_count // (size_x * slab_y))
    block = slab_x * slab_y
    flat = (size_x, slab_y * s.c)
    pert = lax.axis_index("pert").astype(jnp.int32)
    part = lax.axis_index("pw").astype(jnp.int32)
    core = lax.axis_index("band").astype(jnp.int32) & 1
    own_column = lax.broadcasted_iota(jnp.int32, (total_perts, total_perts), 1) == pert
    part, pert, core, own_column, slot = lax.optimization_barrier(
        (part.reshape(1), pert.reshape(1), core.reshape(1), own_column, band_slot)
    )

    table_x = jnp.asarray(left_table(size_x))
    table_y = jnp.asarray(left_table(size_y))
    table_z = jnp.asarray(right_table(size_z))

    def exchange(values):
        return lax.all_to_all(values, "pw", split_axis=0, concat_axis=0, tiled=True)

    psi = psi_coef.reshape(flat)
    index = pw_index.reshape(flat)
    all_psi = lax.all_gather(psi, "band", axis=0)
    anywhere = pl.BlockSpec(memory_space=pltpu.HBM)
    smem = pl.BlockSpec(memory_space=pltpu.SMEM)
    vmem = pl.BlockSpec(memory_space=pltpu.VMEM)
    send, inverse, depth, diag = pl.pallas_call(
        partial(start_kernel, s),
        out_shape=(
            shape(parts, block, size_z),
            shape(slab_y, size_x, size_z, dtype=jnp.int32),
            shape(*flat, dtype=jnp.int32),
            shape(*flat),
        ),
        in_specs=[smem, smem] + [anywhere] * 4,
        out_specs=(vmem,) * 4,
        scratch_shapes=[
            pltpu.SMEM(band_energy.shape, F32),
            pltpu.VMEM(flat, F32),
            pltpu.VMEM(flat, jnp.int32),
            pltpu.VMEM(table_x.shape, BF16),
            pltpu.SemaphoreType.DMA((4,)),
        ],
        compiler_params=pltpu.CompilerParams(vmem_limit_bytes=VMEM_LIMIT),
        name="start",
    )(part, slot, band_energy, psi, index, table_x)
    recv = exchange(send)

    local = local_potential.reshape(slab_x * size_y, size_z)
    trials = trial_potential.reshape(total_perts, slab_x * size_y, size_z)
    send, psi_grid = call(
        partial(band_kernel, s),
        (shape(parts, block, size_z), shape(slab_x * size_y, size_z)),
        0,
        "band",
    )(recv, local, table_y, table_z)
    recv = exchange(send)
    image = call(partial(image_kernel, s), shape(*flat), 0, "image")(recv, depth, table_x)
    all_image = lax.all_gather(image, "band", axis=0)
    psi_grid, image = lax.optimization_barrier((psi_grid, image))
    send = call(partial(driving_kernel, s), shape(parts, block, size_z), 1, "driving")(
        pert, psi_grid, trials, table_y, table_z
    )
    recv = exchange(send)
    driving, dots = call(
        partial(project_kernel, s),
        (shape(*flat), shape(parts, total_bands // 2, size_z)),
        0,
        "project",
    )(recv, depth, all_psi, table_x)
    dots = exchange(dots)
    send, start = call(
        partial(first_kernel, s, coef_total),
        (shape(parts, block, size_z), shape(*flat)),
        0,
        "first",
    )(dots, driving, all_psi, diag, inverse, table_x)
    even, odd = (
        [(i * band_count + b, (1 - i) * band_count + b) for i in range(2) for b in group]
        for group in (range(0, band_count, 2), range(1, band_count, 2))
    )
    for iteration in range(ITERS):
        last = iteration == ITERS - 1
        recv = exchange(send)
        out = shape(parts, block + total_bands // 2, size_z)
        if iteration == 0:
            send = call(partial(apply_potential, s), out, 0, "potential")(
                recv, local, table_y, table_z
            )
            send, driving = lax.optimization_barrier((send, driving))
            other_odd = lax.ppermute(driving, ("pert", "band"), odd)
            send, all_image, driving, other_odd = lax.optimization_barrier(
                (send, all_image, driving, other_odd)
            )
            other_even = lax.ppermute(driving, ("pert", "band"), even)
            send = call(partial(first_dots_kernel, s), out, 0, "dots", {0: 0})(
                send, all_psi, all_image, diag, start
            )
            send, other_even = lax.optimization_barrier((send, other_even))
        else:
            send = call(partial(potential_kernel, s), out, 0, "potential")(
                dots, recv, local, table_y, table_z
            )
        recv = exchange(send)
        if last:
            outs = (shape(parts, block + 8, size_z),)
        else:
            outs = (shape(parts, block, size_z), shape(total_bands // 2, size_z))
        send, *rest = call(partial(update_kernel, s, coef_total, last), outs, 1, "update")(
            pert, recv, start, depth, all_psi, all_image, diag, inverse, table_x, driving,
            other_even, other_odd,
        )
        dots = rest[0] if rest else None

    recv = exchange(send)
    rows = slab_x * (size_y // band_count)
    send = call(
        partial(density_kernel, s, band_count),
        shape(2, band_count // 2, rows + 8, size_z),
        1,
        "density",
    )(core, recv, psi_grid, table_y, table_z)
    got = lax.ppermute(send[1], "band", [(band, band ^ 1) for band in range(band_count)])
    near = [[2 * z + c for z in range(band_count // 2)] for c in range(2)]
    recv = lax.all_to_all(
        send[0] + got, "band", split_axis=0, concat_axis=0, tiled=True, axis_index_groups=near
    )
    density, sums = call(
        partial(final_kernel, s, rows), (shape(rows, size_z), shape(8, size_z)), 0, "final"
    )(recv)
    own = sums[:total_perts, :total_perts] * (2.0 / (total_bands * coef_total))
    across = lax.ppermute(own, "pert", [(0, 1), (1, 0)])
    intersections = jnp.where(own_column, own, across)
    return (
        density.reshape(1, slab_x, size_y // band_count, size_z),
        intersections,
    )


def solution(mesh):
    return jax.shard_map(
        per_device,
        mesh=mesh,
        in_specs=(
            P(None, "pw", None, None),
            P("pw", None, None),
            P("pw", "band"),
            P(),
            P("band"),
            P("pw"),
        ),
        out_specs=(P("pert", "pw", "band", None), P()),
        check_vma=False,
    )
```

```python
import math
from functools import partial

import jax
import jax.numpy as jnp
import numpy as np
from jax import lax
from jax.experimental import pallas as pl
from jax.experimental.pallas import tpu as pltpu
from jax.sharding import PartitionSpec as P

ITERS = 3
F32 = jnp.float32
BF16 = jnp.bfloat16
GROUP = 16
VMEM_LIMIT = 16 * 1024 * 1024


def hartley_pieces(points):
    wave_index = np.arange(points)
    angles = (wave_index[:, None] * wave_index[None, :] % points) * (2.0 * math.pi / points)
    table = (np.cos(angles) + np.sin(angles)) / math.sqrt(points)
    high = table.astype(np.float32).astype(jnp.bfloat16)
    low = (table - high.astype(np.float64)).astype(np.float32).astype(jnp.bfloat16)
    return high, low


def left_table(points):
    high, low = hartley_pieces(points)
    return np.concatenate([high, high, low], axis=1)


def right_table(points):
    high, low = hartley_pieces(points)
    return np.concatenate([high, high, low], axis=0)


def stack_pieces(values, axis):
    high = values.astype(BF16)
    low = (values - high.astype(F32)).astype(BF16)
    return jnp.concatenate([high, low, high], axis=axis)


def from_left(table, values):
    return jnp.dot(table, stack_pieces(values, 0), preferred_element_type=F32)


def all_from_left(table, blocks):
    results = []
    for first in range(0, len(blocks), 2):
        pair = blocks[first : first + 2]
        width = pair[0].shape[1]
        wide = from_left(table, jnp.concatenate(pair, axis=1))
        results += [wide[:, n * width : (n + 1) * width] for n in range(len(pair))]
    return results


def from_right(values, table):
    return jnp.dot(stack_pieces(values, 1), table, preferred_element_type=F32)


def pick(values, lanes):
    return jnp.take_along_axis(values, lanes, axis=1, mode="promise_in_bounds")


def lane_numbers(shape):
    return lax.broadcasted_iota(jnp.int32, shape, len(shape) - 1)


class Sizes:
    def __init__(self, size_x, size_y, size_z, parts, per_line):
        self.x, self.y, self.z, self.parts, self.c = size_x, size_y, size_z, parts, per_line
        self.slab_x, self.slab_y = size_x // parts, size_y // parts


def send_lines(s, flat, inverse_ref, table_x, send_ref):
    placed = []
    for ky in range(s.slab_y):
        lanes = inverse_ref[ky]
        placed.append(jnp.where(lanes >= 0, pick(flat, jnp.maximum(lanes, 0)), 0.0))
    for ky, lines in enumerate(all_from_left(table_x, placed)):
        for part in range(s.parts):
            rows = lines[part * s.slab_x : (part + 1) * s.slab_x]
            send_ref[part, pl.ds(ky, s.slab_x, s.slab_y), :] = rows


def read_lines(s, recv_ref, depth, table_x):
    result = jnp.zeros((s.x, s.slab_y * s.c), F32)
    group = lane_numbers(result.shape) // s.c
    blocks = [
        jnp.concatenate(
            [
                recv_ref[source, pl.ds(ky, s.slab_x, s.slab_y), :]
                for source in range(s.parts)
            ],
            axis=0,
        )
        for ky in range(s.slab_y)
    ]
    for ky, lines in enumerate(all_from_left(table_x, blocks)):
        result = jnp.where(group == ky, pick(lines, depth), result)
    return result


def slabs_in(s, recv_ref, rows, table_y):
    blocks = [
        recv_ref[:, row * s.slab_y : (row + 1) * s.slab_y, :].reshape(s.y, s.z) for row in rows
    ]
    return jnp.concatenate(all_from_left(table_y, blocks), axis=0)


def slabs_out(s, values, table_y, send_ref, rows):
    blocks = [values[n * s.y : (n + 1) * s.y] for n in range(len(rows))]
    for row, lines in zip(rows, all_from_left(table_y, blocks)):
        start = row * s.slab_y
        send_ref[:, start : start + s.slab_y, :] = lines.reshape(s.parts, s.slab_y, s.z)


def fold(dots):
    half = dots.shape[0] // 2
    middle = dots.shape[1] // 2
    folded = dots + pltpu.roll(dots, middle, 1)
    return jnp.where(lane_numbers((half, dots.shape[1])) < middle, folded[:half], folded[half:])


def band_dots(all_bands, flat):
    sums = [
        jnp.sum(all_bands[band] * flat, axis=0, keepdims=True)
        for band in range(all_bands.shape[0])
    ]
    return jnp.concatenate(sums, axis=0)


def band_sum(all_bands, weights):
    total = weights[0:1, :] * all_bands[0]
    for band in range(1, all_bands.shape[0]):
        total = total + weights[band : band + 1, :] * all_bands[band]
    return total


def total_weights(parts, coef_total):
    summed = jnp.sum(parts, axis=0) * (1.0 / coef_total)
    early = lane_numbers(summed.shape) < summed.shape[1] // 2
    halves = [
        jnp.sum(jnp.where(early, summed, 0.0), axis=1, keepdims=True),
        jnp.sum(jnp.where(early, 0.0, summed), axis=1, keepdims=True),
    ]
    weights = jnp.concatenate(halves, axis=0)
    return jnp.broadcast_to(weights, (weights.shape[0], summed.shape[1]))


def wave_energy(wave_number, points):
    folded = jnp.minimum(wave_number, points - wave_number).astype(F32)
    return 4.0 * (folded * (1.0 / points)) ** 2


def start_kernel(s, part_ref, slot_ref, energy_any, psi_any, index_any, tx_any,
                 send_ref, inverse_ref, depth_ref, diag_ref,
                 energy_ref, psi_ref, index_ref, tx_ref, sems):
    copies = [
        pltpu.make_async_copy(source, target, sems.at[number])
        for number, (source, target) in enumerate(
            ((index_any, index_ref), (energy_any, energy_ref), (psi_any, psi_ref), (tx_any, tx_ref))
        )
    ]
    for copy in copies:
        copy.start()
    for copy in copies:
        copy.wait()
    depth = index_ref[...] % s.z
    depth_ref[...] = depth
    turned = depth.T
    cells = lax.broadcasted_iota(jnp.int32, (s.z, s.x), 0)
    for ky in range(s.slab_y):
        inverse = jnp.full((s.z, s.x), -1, jnp.int32)
        for c in range(s.c):
            lane = ky * s.c + c
            inverse = jnp.where(turned[lane : lane + 1, :] == cells, lane, inverse)
        inverse_ref[ky] = inverse.T
    wave_x = lax.broadcasted_iota(jnp.int32, depth.shape, 0)
    wave_y = part_ref[0] * s.slab_y + lane_numbers(depth.shape) // s.c
    kinetic = wave_energy(wave_x, s.x) + wave_energy(wave_y, s.y) + wave_energy(depth, s.z)
    diag_ref[...] = 1.0 / (kinetic - energy_ref[slot_ref[0]])
    send_lines(s, psi_ref[...], inverse_ref, tx_ref[...], send_ref)


def band_kernel(s, recv_ref, local_ref, tyl_ref, tzr_ref, image_ref, grid_ref):
    table_y, table_z = tyl_ref[...], tzr_ref[...]
    group = min(s.slab_x, GROUP)
    for first in range(0, s.slab_x, group):
        inner = slabs_in(s, recv_ref, range(first, first + group), table_y)
        rows = pl.ds(first * s.y, group * s.y)
        grid = from_right(inner, table_z)
        grid_ref[rows, :] = grid
        outer = from_right(local_ref[rows, :] * grid, table_z)
        slabs_out(s, outer, table_y, image_ref, range(first, first + group))


def driving_kernel(s, pert_ref, grid_ref, trial_ref, tyl_ref, tzr_ref, send_ref):
    table_y, table_z = tyl_ref[...], tzr_ref[...]
    group = min(s.slab_x, GROUP)
    for first in range(0, s.slab_x, group):
        rows = pl.ds(first * s.y, group * s.y)
        outer = from_right(trial_ref[pert_ref[0], rows, :] * grid_ref[rows, :], table_z)
        slabs_out(s, outer, table_y, send_ref, range(first, first + group))


def image_kernel(s, recv_ref, depth_ref, tx_ref, image_ref):
    image_ref[...] = read_lines(s, recv_ref, depth_ref[...], tx_ref[...])


def project_kernel(s, recv_ref, depth_ref, all_ref, tx_ref, driving_ref, dots_ref):
    driving = read_lines(s, recv_ref, depth_ref[...], tx_ref[...])
    driving_ref[...] = driving
    dots = fold(band_dots(all_ref, driving))
    dots_ref[...] = jnp.broadcast_to(dots[None], dots_ref.shape)


def first_kernel(s, coef_total, dots_ref, driving_ref, all_ref, diag_ref, inverse_ref,
                 tx_ref, send_ref, start_ref):
    weights = total_weights(dots_ref[...], coef_total)
    start = band_sum(all_ref, weights) - driving_ref[...]
    start_ref[...] = start
    send_lines(s, start * diag_ref[...], inverse_ref, tx_ref[...], send_ref)


def potential_kernel(s, dots_ref, *refs):
    dots = dots_ref[...]
    block = s.slab_x * s.slab_y
    apply_potential(s, *refs)
    refs[-1][:, block:, :] = jnp.broadcast_to(dots[None], (s.parts,) + dots.shape)


def apply_potential(s, recv_ref, local_ref, tyl_ref, tzr_ref, send_ref):
    table_y, table_z = tyl_ref[...], tzr_ref[...]
    group = min(s.slab_x, GROUP)
    for first in range(0, s.slab_x, group):
        inner = slabs_in(s, recv_ref, range(first, first + group), table_y)
        rows = pl.ds(first * s.y, group * s.y)
        grid = from_right(inner, table_z)
        outer = from_right(local_ref[rows, :] * grid, table_z)
        slabs_out(s, outer, table_y, send_ref, range(first, first + group))


def state_dots(bands, images, diag, state):
    return fold(band_dots(bands, state) + band_dots(images, diag * state))


def first_dots_kernel(s, held_ref, all_ref, image_ref, diag_ref, start_ref, send_ref):
    dots = state_dots(all_ref, image_ref, diag_ref[...], start_ref[...])
    block = s.slab_x * s.slab_y
    send_ref[:, block:, :] = jnp.broadcast_to(dots[None], (s.parts,) + dots.shape)


def update_kernel(s, coef_total, last, pert_ref, recv_ref, start_ref, depth_ref, all_ref,
                  image_ref, diag_ref, inverse_ref, tx_ref, own_ref, other_ref, send_ref, dots_ref=None):
    block = s.slab_x * s.slab_y
    table_x = tx_ref[...]
    weights = total_weights(recv_ref[:, block:, :], coef_total)
    change = read_lines(s, recv_ref, depth_ref[...], table_x)
    diag = diag_ref[...]
    state = start_ref[...] - change + band_sum(all_ref, weights)
    response = state * diag
    send_lines(s, response, inverse_ref, table_x, send_ref)
    if not last:
        dots_ref[...] = state_dots(all_ref, image_ref, diag, state)
        return
    own = jnp.sum(own_ref[...] * response, axis=0, keepdims=True)
    other = jnp.sum(other_ref[...] * response, axis=0, keepdims=True)
    lead = pert_ref[0] == 0
    rest = jnp.zeros((6, own.shape[1]), F32)
    sums = jnp.concatenate(
        [jnp.where(lead, own, other), jnp.where(lead, other, own), rest], axis=0
    )
    send_ref[:, block:, :] = jnp.broadcast_to(sums[None], (s.parts,) + sums.shape)


def density_kernel(s, bands, core_ref, recv_ref, grid_ref, tyl_ref, tzr_ref, send_ref):
    table_y, table_z = tyl_ref[...], tzr_ref[...]
    group = min(s.slab_x, GROUP)
    keep = s.y // bands
    for first in range(0, s.slab_x, group):
        inner = slabs_in(s, recv_ref, range(first, first + group), table_y)
        rows = pl.ds(first * s.y, group * s.y)
        density = 2.0 * grid_ref[rows, :] * from_right(inner, table_z)
        for row in range(group):
            for band in range(bands):
                start = row * s.y + band * keep
                place = (first + row) * keep
                slot = core_ref[0] if band % 2 == 0 else 1 - core_ref[0]
                send_ref[slot, band // 2, place : place + keep, :] = density[start : start + keep]
    sums = jnp.sum(recv_ref[:, s.slab_x * s.slab_y :, :], axis=0)
    send_ref[:, :, s.slab_x * keep :, :] = jnp.broadcast_to(
        sums[None, None], (2, bands // 2) + sums.shape
    )


def final_kernel(s, rows, recv_ref, density_ref, sums_ref):
    total = jnp.sum(recv_ref[...], axis=0)
    density_ref[...] = total[:rows]
    lanes = jnp.sum(total[rows:], axis=1, keepdims=True)
    sums_ref[...] = jnp.broadcast_to(lanes, sums_ref.shape)


def call(kernel, out_shape, scalars=0, name=None, aliases=None):
    smem = pl.BlockSpec(memory_space=pltpu.SMEM)
    vmem = pl.BlockSpec(memory_space=pltpu.VMEM)

    def run(*operands):
        return pl.pallas_call(
            kernel,
            out_shape=out_shape,
            in_specs=[smem] * scalars + [vmem] * (len(operands) - scalars),
            out_specs=jax.tree.map(lambda _: vmem, out_shape),
            compiler_params=pltpu.CompilerParams(vmem_limit_bytes=VMEM_LIMIT),
            input_output_aliases=aliases or {},
            name=name,
        )(*operands)

    return run


def shape(*sizes, dtype=F32):
    return jax.ShapeDtypeStruct(sizes, dtype)


def per_device(trial_potential, local_potential, psi_coef, band_energy, band_slot, pw_index):
    parts = lax.axis_size("pw")
    band_count = lax.axis_size("band")
    slab_x, size_y, size_z = local_potential.shape
    size_x = slab_x * parts
    coef_count = psi_coef.shape[0]
    coef_total = coef_count * parts
    total_bands = band_energy.shape[0]
    total_perts = trial_potential.shape[0]
    slab_y = size_y // parts
    s = Sizes(size_x, size_y, size_z, parts, coef_count // (size_x * slab_y))
    block = slab_x * slab_y
    flat = (size_x, slab_y * s.c)
    pert = lax.axis_index("pert").astype(jnp.int32)
    part = lax.axis_index("pw").astype(jnp.int32)
    core = lax.axis_index("band").astype(jnp.int32) & 1
    own_column = lax.broadcasted_iota(jnp.int32, (total_perts, total_perts), 1) == pert
    part, pert, core, own_column, slot = lax.optimization_barrier(
        (part.reshape(1), pert.reshape(1), core.reshape(1), own_column, band_slot)
    )

    table_x = jnp.asarray(left_table(size_x))
    table_y = jnp.asarray(left_table(size_y))
    table_z = jnp.asarray(right_table(size_z))

    def exchange(values):
        return lax.all_to_all(values, "pw", split_axis=0, concat_axis=0, tiled=True)

    psi = psi_coef.reshape(flat)
    index = pw_index.reshape(flat)
    all_psi = lax.all_gather(psi, "band", axis=0)
    anywhere = pl.BlockSpec(memory_space=pltpu.HBM)
    smem = pl.BlockSpec(memory_space=pltpu.SMEM)
    vmem = pl.BlockSpec(memory_space=pltpu.VMEM)
    send, inverse, depth, diag = pl.pallas_call(
        partial(start_kernel, s),
        out_shape=(
            shape(parts, block, size_z),
            shape(slab_y, size_x, size_z, dtype=jnp.int32),
            shape(*flat, dtype=jnp.int32),
            shape(*flat),
        ),
        in_specs=[smem, smem] + [anywhere] * 4,
        out_specs=(vmem,) * 4,
        scratch_shapes=[
            pltpu.SMEM(band_energy.shape, F32),
            pltpu.VMEM(flat, F32),
            pltpu.VMEM(flat, jnp.int32),
            pltpu.VMEM(table_x.shape, BF16),
            pltpu.SemaphoreType.DMA((4,)),
        ],
        compiler_params=pltpu.CompilerParams(vmem_limit_bytes=VMEM_LIMIT),
        name="start",
    )(part, slot, band_energy, psi, index, table_x)
    recv = exchange(send)

    local = local_potential.reshape(slab_x * size_y, size_z)
    trials = trial_potential.reshape(total_perts, slab_x * size_y, size_z)
    send, psi_grid = call(
        partial(band_kernel, s),
        (shape(parts, block, size_z), shape(slab_x * size_y, size_z)),
        0,
        "band",
    )(recv, local, table_y, table_z)
    recv = exchange(send)
    image = call(partial(image_kernel, s), shape(*flat), 0, "image")(recv, depth, table_x)
    all_image = lax.all_gather(image, "band", axis=0)
    psi_grid, image = lax.optimization_barrier((psi_grid, image))
    send = call(partial(driving_kernel, s), shape(parts, block, size_z), 1, "driving")(
        pert, psi_grid, trials, table_y, table_z
    )
    recv = exchange(send)
    driving, dots = call(
        partial(project_kernel, s),
        (shape(*flat), shape(parts, total_bands // 2, size_z)),
        0,
        "project",
    )(recv, depth, all_psi, table_x)
    dots = exchange(dots)
    send, start = call(
        partial(first_kernel, s, coef_total),
        (shape(parts, block, size_z), shape(*flat)),
        0,
        "first",
    )(dots, driving, all_psi, diag, inverse, table_x)
    for iteration in range(ITERS):
        last = iteration == ITERS - 1
        recv = exchange(send)
        out = shape(parts, block + total_bands // 2, size_z)
        if iteration == 0:
            send = call(partial(apply_potential, s), out, 0, "potential")(
                recv, local, table_y, table_z
            )
            send, driving = lax.optimization_barrier((send, driving))
            other = lax.ppermute(driving, "pert", [(0, 1), (1, 0)])
            send, all_image, other = lax.optimization_barrier((send, all_image, other))
            send = call(partial(first_dots_kernel, s), out, 0, "dots", {0: 0})(
                send, all_psi, all_image, diag, start
            )
        else:
            send = call(partial(potential_kernel, s), out, 0, "potential")(
                dots, recv, local, table_y, table_z
            )
        recv = exchange(send)
        if last:
            outs = (shape(parts, block + 8, size_z),)
        else:
            outs = (shape(parts, block, size_z), shape(total_bands // 2, size_z))
        send, *rest = call(partial(update_kernel, s, coef_total, last), outs, 1, "update")(
            pert, recv, start, depth, all_psi, all_image, diag, inverse, table_x, driving,
            other,
        )
        dots = rest[0] if rest else None

    recv = exchange(send)
    rows = slab_x * (size_y // band_count)
    send = call(
        partial(density_kernel, s, band_count),
        shape(2, band_count // 2, rows + 8, size_z),
        1,
        "density",
    )(core, recv, psi_grid, table_y, table_z)
    got = lax.ppermute(send[1], "band", [(band, band ^ 1) for band in range(band_count)])
    near = [[2 * z + c for z in range(band_count // 2)] for c in range(2)]
    recv = lax.all_to_all(
        send[0] + got, "band", split_axis=0, concat_axis=0, tiled=True, axis_index_groups=near
    )
    density, sums = call(
        partial(final_kernel, s, rows), (shape(rows, size_z), shape(8, size_z)), 0, "final"
    )(recv)
    own = sums[:total_perts, :total_perts] * (2.0 / (total_bands * coef_total))
    across = lax.ppermute(own, "pert", [(0, 1), (1, 0)])
    intersections = jnp.where(own_column, own, across)
    return (
        density.reshape(1, slab_x, size_y // band_count, size_z),
        intersections,
    )


def solution(mesh):
    return jax.shard_map(
        per_device,
        mesh=mesh,
        in_specs=(
            P(None, "pw", None, None),
            P("pw", None, None),
            P("pw", "band"),
            P(),
            P("band"),
            P("pw"),
        ),
        out_specs=(P("pert", "pw", "band", None), P()),
        check_vma=False,
    )
```

```python
import math
from functools import partial

import jax
import jax.numpy as jnp
import numpy as np
from jax import lax
from jax.experimental import pallas as pl
from jax.experimental.pallas import tpu as pltpu
from jax.sharding import PartitionSpec as P

ITERS = 3
F32 = jnp.float32
BF16 = jnp.bfloat16
GROUP = 16
VMEM_LIMIT = 16 * 1024 * 1024


def hartley_pieces(points):
    wave_index = np.arange(points)
    angles = (wave_index[:, None] * wave_index[None, :] % points) * (2.0 * math.pi / points)
    table = (np.cos(angles) + np.sin(angles)) / math.sqrt(points)
    high = table.astype(np.float32).astype(jnp.bfloat16)
    low = (table - high.astype(np.float64)).astype(np.float32).astype(jnp.bfloat16)
    return high, low


def left_table(points):
    high, low = hartley_pieces(points)
    return np.concatenate([high, high, low], axis=1)


def right_table(points):
    high, low = hartley_pieces(points)
    return np.concatenate([high, high, low], axis=0)


def stack_pieces(values, axis):
    high = values.astype(BF16)
    low = (values - high.astype(F32)).astype(BF16)
    return jnp.concatenate([high, low, high], axis=axis)


def from_left(table, values):
    return jnp.dot(table, stack_pieces(values, 0), preferred_element_type=F32)


def all_from_left(table, blocks):
    results = []
    for first in range(0, len(blocks), 2):
        pair = blocks[first : first + 2]
        width = pair[0].shape[1]
        wide = from_left(table, jnp.concatenate(pair, axis=1))
        results += [wide[:, n * width : (n + 1) * width] for n in range(len(pair))]
    return results


def from_right(values, table):
    return jnp.dot(stack_pieces(values, 1), table, preferred_element_type=F32)


def pick(values, lanes):
    return jnp.take_along_axis(values, lanes, axis=1, mode="promise_in_bounds")


def lane_numbers(shape):
    return lax.broadcasted_iota(jnp.int32, shape, len(shape) - 1)


class Sizes:
    def __init__(self, size_x, size_y, size_z, parts, per_line):
        self.x, self.y, self.z, self.parts, self.c = size_x, size_y, size_z, parts, per_line
        self.slab_x, self.slab_y = size_x // parts, size_y // parts


def send_lines(s, flat, inverse_ref, table_x, send_ref):
    placed = []
    for ky in range(s.slab_y):
        lanes = inverse_ref[ky]
        placed.append(jnp.where(lanes >= 0, pick(flat, jnp.maximum(lanes, 0)), 0.0))
    for ky, lines in enumerate(all_from_left(table_x, placed)):
        for part in range(s.parts):
            rows = lines[part * s.slab_x : (part + 1) * s.slab_x]
            send_ref[part, pl.ds(ky, s.slab_x, s.slab_y), :] = rows


def read_lines(s, recv_ref, depth, table_x):
    result = jnp.zeros((s.x, s.slab_y * s.c), F32)
    group = lane_numbers(result.shape) // s.c
    blocks = [
        jnp.concatenate(
            [
                recv_ref[source, pl.ds(ky, s.slab_x, s.slab_y), :]
                for source in range(s.parts)
            ],
            axis=0,
        )
        for ky in range(s.slab_y)
    ]
    for ky, lines in enumerate(all_from_left(table_x, blocks)):
        result = jnp.where(group == ky, pick(lines, depth), result)
    return result


def slabs_in(s, recv_ref, rows, table_y):
    blocks = [
        recv_ref[:, row * s.slab_y : (row + 1) * s.slab_y, :].reshape(s.y, s.z) for row in rows
    ]
    return jnp.concatenate(all_from_left(table_y, blocks), axis=0)


def slabs_out(s, values, table_y, send_ref, rows):
    blocks = [values[n * s.y : (n + 1) * s.y] for n in range(len(rows))]
    for row, lines in zip(rows, all_from_left(table_y, blocks)):
        start = row * s.slab_y
        send_ref[:, start : start + s.slab_y, :] = lines.reshape(s.parts, s.slab_y, s.z)


def fold(dots):
    half = dots.shape[0] // 2
    middle = dots.shape[1] // 2
    folded = dots + pltpu.roll(dots, middle, 1)
    return jnp.where(lane_numbers((half, dots.shape[1])) < middle, folded[:half], folded[half:])


def band_dots(all_bands, flat):
    sums = [
        jnp.sum(all_bands[band] * flat, axis=0, keepdims=True)
        for band in range(all_bands.shape[0])
    ]
    return jnp.concatenate(sums, axis=0)


def band_sum(all_bands, weights):
    total = weights[0:1, :] * all_bands[0]
    for band in range(1, all_bands.shape[0]):
        total = total + weights[band : band + 1, :] * all_bands[band]
    return total


def total_weights(parts, coef_total):
    summed = jnp.sum(parts, axis=0) * (1.0 / coef_total)
    early = lane_numbers(summed.shape) < summed.shape[1] // 2
    halves = [
        jnp.sum(jnp.where(early, summed, 0.0), axis=1, keepdims=True),
        jnp.sum(jnp.where(early, 0.0, summed), axis=1, keepdims=True),
    ]
    weights = jnp.concatenate(halves, axis=0)
    return jnp.broadcast_to(weights, (weights.shape[0], summed.shape[1]))


def wave_energy(wave_number, points):
    folded = jnp.minimum(wave_number, points - wave_number).astype(F32)
    return 4.0 * (folded * (1.0 / points)) ** 2


def start_kernel(s, part_ref, slot_ref, energy_any, psi_any, index_any, tx_any,
                 send_ref, inverse_ref, depth_ref, diag_ref,
                 energy_ref, psi_ref, index_ref, tx_ref, sems):
    copies = [
        pltpu.make_async_copy(source, target, sems.at[number])
        for number, (source, target) in enumerate(
            ((index_any, index_ref), (energy_any, energy_ref), (psi_any, psi_ref), (tx_any, tx_ref))
        )
    ]
    for copy in copies:
        copy.start()
    for copy in copies:
        copy.wait()
    depth = index_ref[...] % s.z
    depth_ref[...] = depth
    turned = depth.T
    cells = lax.broadcasted_iota(jnp.int32, (s.z, s.x), 0)
    for ky in range(s.slab_y):
        inverse = jnp.full((s.z, s.x), -1, jnp.int32)
        for c in range(s.c):
            lane = ky * s.c + c
            inverse = jnp.where(turned[lane : lane + 1, :] == cells, lane, inverse)
        inverse_ref[ky] = inverse.T
    wave_x = lax.broadcasted_iota(jnp.int32, depth.shape, 0)
    wave_y = part_ref[0] * s.slab_y + lane_numbers(depth.shape) // s.c
    kinetic = wave_energy(wave_x, s.x) + wave_energy(wave_y, s.y) + wave_energy(depth, s.z)
    diag_ref[...] = 1.0 / (kinetic - energy_ref[slot_ref[0]])
    send_lines(s, psi_ref[...], inverse_ref, tx_ref[...], send_ref)


def band_kernel(s, recv_ref, local_ref, tyl_ref, tzr_ref, image_ref, grid_ref):
    table_y, table_z = tyl_ref[...], tzr_ref[...]
    group = min(s.slab_x, GROUP)
    for first in range(0, s.slab_x, group):
        inner = slabs_in(s, recv_ref, range(first, first + group), table_y)
        rows = pl.ds(first * s.y, group * s.y)
        grid = from_right(inner, table_z)
        grid_ref[rows, :] = grid
        outer = from_right(local_ref[rows, :] * grid, table_z)
        slabs_out(s, outer, table_y, image_ref, range(first, first + group))


def driving_kernel(s, pert_ref, grid_ref, trial_ref, tyl_ref, tzr_ref, send_ref):
    table_y, table_z = tyl_ref[...], tzr_ref[...]
    group = min(s.slab_x, GROUP)
    for first in range(0, s.slab_x, group):
        rows = pl.ds(first * s.y, group * s.y)
        outer = from_right(trial_ref[pert_ref[0], rows, :] * grid_ref[rows, :], table_z)
        slabs_out(s, outer, table_y, send_ref, range(first, first + group))


def image_kernel(s, recv_ref, depth_ref, tx_ref, image_ref):
    image_ref[...] = read_lines(s, recv_ref, depth_ref[...], tx_ref[...])


def project_kernel(s, recv_ref, depth_ref, all_ref, tx_ref, driving_ref, dots_ref):
    driving = read_lines(s, recv_ref, depth_ref[...], tx_ref[...])
    driving_ref[...] = driving
    dots = fold(band_dots(all_ref, driving))
    dots_ref[...] = jnp.broadcast_to(dots[None], dots_ref.shape)


def first_kernel(s, coef_total, dots_ref, driving_ref, all_ref, diag_ref, inverse_ref,
                 tx_ref, send_ref, start_ref):
    weights = total_weights(dots_ref[...], coef_total)
    start = band_sum(all_ref, weights) - driving_ref[...]
    start_ref[...] = start
    send_lines(s, start * diag_ref[...], inverse_ref, tx_ref[...], send_ref)


def potential_kernel(s, dots_ref, *refs):
    dots = dots_ref[...]
    block = s.slab_x * s.slab_y
    apply_potential(s, *refs)
    refs[-1][:, block:, :] = jnp.broadcast_to(dots[None], (s.parts,) + dots.shape)


def apply_potential(s, recv_ref, local_ref, tyl_ref, tzr_ref, send_ref):
    table_y, table_z = tyl_ref[...], tzr_ref[...]
    group = min(s.slab_x, GROUP)
    for first in range(0, s.slab_x, group):
        inner = slabs_in(s, recv_ref, range(first, first + group), table_y)
        rows = pl.ds(first * s.y, group * s.y)
        grid = from_right(inner, table_z)
        outer = from_right(local_ref[rows, :] * grid, table_z)
        slabs_out(s, outer, table_y, send_ref, range(first, first + group))


def state_dots(bands, images, diag, state):
    return fold(band_dots(bands, state) + band_dots(images, diag * state))


def first_potential_kernel(s, start_ref, recv_ref, local_ref, tyl_ref, tzr_ref, send_ref,
                           kept_ref):
    kept_ref[...] = start_ref[...]
    apply_potential(s, recv_ref, local_ref, tyl_ref, tzr_ref, send_ref)


def first_dots_kernel(s, held_ref, all_ref, image_ref, diag_ref, start_ref, send_ref):
    dots = state_dots(all_ref, image_ref, diag_ref[...], start_ref[...])
    block = s.slab_x * s.slab_y
    send_ref[:, block:, :] = jnp.broadcast_to(dots[None], (s.parts,) + dots.shape)


def update_kernel(s, coef_total, last, pert_ref, recv_ref, start_ref, depth_ref, all_ref,
                  image_ref, diag_ref, inverse_ref, tx_ref, own_ref, other_ref, send_ref, dots_ref=None):
    block = s.slab_x * s.slab_y
    table_x = tx_ref[...]
    weights = total_weights(recv_ref[:, block:, :], coef_total)
    change = read_lines(s, recv_ref, depth_ref[...], table_x)
    diag = diag_ref[...]
    state = start_ref[...] - change + band_sum(all_ref, weights)
    response = state * diag
    send_lines(s, response, inverse_ref, table_x, send_ref)
    if not last:
        dots_ref[...] = state_dots(all_ref, image_ref, diag, state)
        return
    own = jnp.sum(own_ref[...] * response, axis=0, keepdims=True)
    other = jnp.sum(other_ref[...] * response, axis=0, keepdims=True)
    lead = pert_ref[0] == 0
    rest = jnp.zeros((6, own.shape[1]), F32)
    sums = jnp.concatenate(
        [jnp.where(lead, own, other), jnp.where(lead, other, own), rest], axis=0
    )
    send_ref[:, block:, :] = jnp.broadcast_to(sums[None], (s.parts,) + sums.shape)


def density_kernel(s, bands, core_ref, recv_ref, grid_ref, tyl_ref, tzr_ref, send_ref):
    table_y, table_z = tyl_ref[...], tzr_ref[...]
    group = min(s.slab_x, GROUP)
    keep = s.y // bands
    for first in range(0, s.slab_x, group):
        inner = slabs_in(s, recv_ref, range(first, first + group), table_y)
        rows = pl.ds(first * s.y, group * s.y)
        density = 2.0 * grid_ref[rows, :] * from_right(inner, table_z)
        for row in range(group):
            for band in range(bands):
                start = row * s.y + band * keep
                place = (first + row) * keep
                slot = core_ref[0] if band % 2 == 0 else 1 - core_ref[0]
                send_ref[slot, band // 2, place : place + keep, :] = density[start : start + keep]
    sums = jnp.sum(recv_ref[:, s.slab_x * s.slab_y :, :], axis=0)
    send_ref[:, :, s.slab_x * keep :, :] = jnp.broadcast_to(
        sums[None, None], (2, bands // 2) + sums.shape
    )


def final_kernel(s, rows, recv_ref, density_ref, sums_ref):
    total = jnp.sum(recv_ref[...], axis=0)
    density_ref[...] = total[:rows]
    lanes = jnp.sum(total[rows:], axis=1, keepdims=True)
    sums_ref[...] = jnp.broadcast_to(lanes, sums_ref.shape)


def call(kernel, out_shape, scalars=0, name=None, aliases=None):
    smem = pl.BlockSpec(memory_space=pltpu.SMEM)
    vmem = pl.BlockSpec(memory_space=pltpu.VMEM)

    def run(*operands):
        return pl.pallas_call(
            kernel,
            out_shape=out_shape,
            in_specs=[smem] * scalars + [vmem] * (len(operands) - scalars),
            out_specs=jax.tree.map(lambda _: vmem, out_shape),
            compiler_params=pltpu.CompilerParams(vmem_limit_bytes=VMEM_LIMIT),
            input_output_aliases=aliases or {},
            name=name,
        )(*operands)

    return run


def shape(*sizes, dtype=F32):
    return jax.ShapeDtypeStruct(sizes, dtype)


def per_device(trial_potential, local_potential, psi_coef, band_energy, band_slot, pw_index):
    parts = lax.axis_size("pw")
    band_count = lax.axis_size("band")
    slab_x, size_y, size_z = local_potential.shape
    size_x = slab_x * parts
    coef_count = psi_coef.shape[0]
    coef_total = coef_count * parts
    total_bands = band_energy.shape[0]
    total_perts = trial_potential.shape[0]
    slab_y = size_y // parts
    s = Sizes(size_x, size_y, size_z, parts, coef_count // (size_x * slab_y))
    block = slab_x * slab_y
    flat = (size_x, slab_y * s.c)
    pert = lax.axis_index("pert").astype(jnp.int32)
    part = lax.axis_index("pw").astype(jnp.int32)
    core = lax.axis_index("band").astype(jnp.int32) & 1
    own_column = lax.broadcasted_iota(jnp.int32, (total_perts, total_perts), 1) == pert
    part, pert, core, own_column, slot = lax.optimization_barrier(
        (part.reshape(1), pert.reshape(1), core.reshape(1), own_column, band_slot)
    )

    table_x = jnp.asarray(left_table(size_x))
    table_y = jnp.asarray(left_table(size_y))
    table_z = jnp.asarray(right_table(size_z))

    def exchange(values):
        return lax.all_to_all(values, "pw", split_axis=0, concat_axis=0, tiled=True)

    psi = psi_coef.reshape(flat)
    index = pw_index.reshape(flat)
    all_psi = lax.all_gather(psi, "band", axis=0)
    anywhere = pl.BlockSpec(memory_space=pltpu.HBM)
    smem = pl.BlockSpec(memory_space=pltpu.SMEM)
    vmem = pl.BlockSpec(memory_space=pltpu.VMEM)
    send, inverse, depth, diag = pl.pallas_call(
        partial(start_kernel, s),
        out_shape=(
            shape(parts, block, size_z),
            shape(slab_y, size_x, size_z, dtype=jnp.int32),
            shape(*flat, dtype=jnp.int32),
            shape(*flat),
        ),
        in_specs=[smem, smem] + [anywhere] * 4,
        out_specs=(vmem,) * 4,
        scratch_shapes=[
            pltpu.SMEM(band_energy.shape, F32),
            pltpu.VMEM(flat, F32),
            pltpu.VMEM(flat, jnp.int32),
            pltpu.VMEM(table_x.shape, BF16),
            pltpu.SemaphoreType.DMA((4,)),
        ],
        compiler_params=pltpu.CompilerParams(vmem_limit_bytes=VMEM_LIMIT),
        name="start",
    )(part, slot, band_energy, psi, index, table_x)
    recv = exchange(send)

    local = local_potential.reshape(slab_x * size_y, size_z)
    trials = trial_potential.reshape(total_perts, slab_x * size_y, size_z)
    send, psi_grid = call(
        partial(band_kernel, s),
        (shape(parts, block, size_z), shape(slab_x * size_y, size_z)),
        0,
        "band",
    )(recv, local, table_y, table_z)
    recv = exchange(send)
    image = call(partial(image_kernel, s), shape(*flat), 0, "image")(recv, depth, table_x)
    all_image = lax.all_gather(image, "band", axis=0)
    psi_grid, image = lax.optimization_barrier((psi_grid, image))
    send = call(partial(driving_kernel, s), shape(parts, block, size_z), 1, "driving")(
        pert, psi_grid, trials, table_y, table_z
    )
    recv = exchange(send)
    driving, dots = call(
        partial(project_kernel, s),
        (shape(*flat), shape(parts, total_bands // 2, size_z)),
        0,
        "project",
    )(recv, depth, all_psi, table_x)
    dots = exchange(dots)
    send, start = call(
        partial(first_kernel, s, coef_total),
        (shape(parts, block, size_z), shape(*flat)),
        0,
        "first",
    )(dots, driving, all_psi, diag, inverse, table_x)
    for iteration in range(ITERS):
        last = iteration == ITERS - 1
        recv = exchange(send)
        out = shape(parts, block + total_bands // 2, size_z)
        if iteration == 0:
            send, kept = call(
                partial(first_potential_kernel, s), (out, shape(*flat)), 0, "potential"
            )(start, recv, local, table_y, table_z)
            send, driving = lax.optimization_barrier((send, driving))
            other = lax.ppermute(driving, "pert", [(0, 1), (1, 0)])
            send, all_image, other = lax.optimization_barrier((send, all_image, other))
            send = call(partial(first_dots_kernel, s), out, 0, "dots", {0: 0})(
                send, all_psi, all_image, diag, kept
            )
        else:
            send = call(partial(potential_kernel, s), out, 0, "potential")(
                dots, recv, local, table_y, table_z
            )
        recv = exchange(send)
        if last:
            outs = (shape(parts, block + 8, size_z),)
        else:
            outs = (shape(parts, block, size_z), shape(total_bands // 2, size_z))
        send, *rest = call(partial(update_kernel, s, coef_total, last), outs, 1, "update")(
            pert, recv, start, depth, all_psi, all_image, diag, inverse, table_x, driving,
            other,
        )
        dots = rest[0] if rest else None

    recv = exchange(send)
    rows = slab_x * (size_y // band_count)
    send = call(
        partial(density_kernel, s, band_count),
        shape(2, band_count // 2, rows + 8, size_z),
        1,
        "density",
    )(core, recv, psi_grid, table_y, table_z)
    got = lax.ppermute(send[1], "band", [(band, band ^ 1) for band in range(band_count)])
    near = [[2 * z + c for z in range(band_count // 2)] for c in range(2)]
    recv = lax.all_to_all(
        send[0] + got, "band", split_axis=0, concat_axis=0, tiled=True, axis_index_groups=near
    )
    density, sums = call(
        partial(final_kernel, s, rows), (shape(rows, size_z), shape(8, size_z)), 0, "final"
    )(recv)
    own = sums[:total_perts, :total_perts] * (2.0 / (total_bands * coef_total))
    across = lax.ppermute(own, "pert", [(0, 1), (1, 0)])
    intersections = jnp.where(own_column, own, across)
    return (
        density.reshape(1, slab_x, size_y // band_count, size_z),
        intersections,
    )


def solution(mesh):
    return jax.shard_map(
        per_device,
        mesh=mesh,
        in_specs=(
            P(None, "pw", None, None),
            P("pw", None, None),
            P("pw", "band"),
            P(),
            P("band"),
            P("pw"),
        ),
        out_specs=(P("pert", "pw", "band", None), P()),
        check_vma=False,
    )
```
